512 devices in a mesh: turn: 64 (over y, z_lo, core), head: 8 (over z_hi, x).
Axes of the slice: x: 4, y: 4, z: 16 (z_hi: 2, z_lo: 8; z = z_hi * 8 + z_lo), core: 2. Of those that a mesh axis runs over, the one named last changes fastest.
Arguments:
- query: bfloat16 [32768, 8192], P('turn', 'head'), may hold values from -6 to 6
- vision: bfloat16 [1024, 8192], P(None, 'turn'), may hold values from -6 to 6
- w_key: bfloat16 [8192, 1024], P('turn', 'head'), may hold values from -0.0625 to 0.0625
- w_value: bfloat16 [8192, 1024], P('turn', 'head'), may hold values from -0.0625 to 0.0625
- q_gain: float32 [128], replicated, may hold values from 0.8 to 2.2
- k_gain: float32 [128], replicated, may hold values from 0.8 to 2.2
- text_turn: int32 [32768], P('turn'), may hold values from 0 to 63, never falling along the last dimension, each value on 1 to 1024 neighbouring positions
- tile_turn: int32 [4], replicated, may hold values from 0 to 63, as said below
- tile_len: int32 [4], replicated, may hold values from 128 to 256, as said below
- grad_out: bfloat16 [32768, 8192], P('turn', 'head'), may hold values from -6 to 6
Outputs:
- attended: bfloat16 [32768, 8192], P('turn', 'head')
- grad_query: bfloat16 [32768, 8192], P('turn', 'head')
- grad_vision: bfloat16 [1024, 8192], P('head', 'turn')
- grad_w_key: float32 [8192, 1024], P('turn', 'head')
- grad_w_value: float32 [8192, 1024], P('turn', 'head')
The draws below stay inside these ranges and needn't reach their ends.
Inputs may be any that keep to these rules, and one draw needn't show every extreme that they name: `text_turn`: never falling along the dialogue; every turn holds 1 to 1024 tokens. `tile_turn`: some tile is shown at turn 0. `tile_len`: some tile is full.
All inputs are finite; a program needn't handle non-finite values.
Results may differ from the reference program's by a relative error of at most 0.02.
Values may be sent and summed in bfloat16 or wider, within the bound.
A program may use at most 64 MiB of HBM per device.

```python
import math
import jax
import jax.numpy as jnp
import numpy as np
from jax import lax

D = 8192
HEADS = 64
KV_HEADS = 8
HD = 128
TILES = 4
TILE_TOK = 256
TURNS = 64
TEXT = 32768
VIS = 1024


def draw_tile_turn(key, part):
    key = jax.random.fold_in(key, 11)
    first, second = jax.random.split(key)
    turns = jax.random.randint(first, (TILES,), 0, TURNS, dtype=jnp.int32)
    order = jax.random.permutation(second, TILES)
    turns = turns.at[order[0]].set(0)
    turns = turns.at[order[1]].set(TURNS - 1)
    return turns


def draw_tile_len(key, part):
    key = jax.random.fold_in(key, 23)
    first, second = jax.random.split(key)
    lengths = jax.random.randint(first, (TILES,), TILE_TOK // 2, TILE_TOK + 1, dtype=jnp.int32)
    order = jax.random.permutation(second, TILES)
    lengths = lengths.at[order[0]].set(TILE_TOK)
    lengths = lengths.at[order[1]].set(TILE_TOK // 2)
    return lengths


def levels(key, dims, shards, low, largest):
    level, own = 1.0, jax.random.fold_in(key, 6)
    for dim, shards_of in shards:
        draws = jnp.exp(jax.random.uniform(jax.random.fold_in(own, dim), (shards_of,), jnp.float32, low / len(shards), largest / len(shards)))
        level = level * jnp.repeat(draws, dims[dim] // shards_of).reshape([-1 if axis == dim else 1 for axis in range(len(dims))])
    return level


def length_profile(number_of, total, bound, skew):
    loads = [(1 << 20) // math.isqrt(rank ** skew) + 1 for rank in range(2, number_of + 1)]
    rest, counts = total - bound - (number_of - 1), [1] * (number_of - 1)
    while rest > 0:
        candidates = [i for i in range(number_of - 1) if counts[i] < bound]
        pool, remaining = sum([loads[i] for i in candidates]), rest
        for i in candidates:
            addition = min(bound - counts[i], max(1, remaining * loads[i] // pool), rest)
            counts[i] = counts[i] + addition
            rest = rest - addition
    return np.array([bound] + counts)


def uneven_parts(own_key, count, total, reach, slope):
    if count == 2:
        one = jax.random.randint(own_key, (), max(1, total - reach), min(reach, total - 1) + 1)
        return jnp.stack([one, total - one])
    sizes = jnp.asarray(length_profile(count, total, reach, slope), jnp.int32)
    couples = (count - 1) // 2
    donor, taker = sizes[1:1 + 2 * couples:2], sizes[2:2 + 2 * couples:2]
    room = jnp.minimum(donor - 1, reach - taker)
    passed = jax.random.randint(jax.random.fold_in(own_key, 1), (couples,), 0, 1 << 20) % (room + 1)
    sizes = sizes.at[1:1 + 2 * couples:2].set(donor - passed).at[2:2 + 2 * couples:2].set(taker + passed)
    return sizes[jax.random.permutation(jax.random.fold_in(own_key, 2), count)]


def normal_values(key, dims, scale, bound, cuts=(), kind=jnp.bfloat16):
    values = scale * jax.random.normal(key, dims, jnp.float32)
    if cuts:
        values = values * levels(key, dims, cuts, -0.22, 0.18)
    return jnp.clip(values, -bound, bound).astype(kind)


def setup_inputs(seed: int = 0) -> dict:
    key_list = jax.random.split(jax.random.key(seed), 11)
    return {
        "query": normal_values(key_list[0], (TEXT, HEADS * HD), 1.0, 6.0, ((0, 64), (1, 8))),
        "vision": normal_values(key_list[1], (VIS, D), 1.0, 6.0, ((1, 64),)),
        "w_key": normal_values(key_list[2], (D, KV_HEADS * HD), D ** -0.5, 0.0625, ((0, 64), (1, 8))),
        "w_value": normal_values(key_list[3], (D, KV_HEADS * HD), D ** -0.5, 0.0625, ((0, 64), (1, 8))),
        "q_gain": jnp.clip(jnp.exp(jax.random.uniform(key_list[4], (HD,), jnp.float32, math.log(0.8), math.log(2.2))), 0.8, 2.2),
        "k_gain": jnp.clip(jnp.exp(jax.random.uniform(key_list[5], (HD,), jnp.float32, math.log(0.8), math.log(2.2))), 0.8, 2.2),
        "text_turn": jnp.searchsorted(jnp.cumsum(uneven_parts(key_list[6], TURNS, TEXT, 2 * TEXT // TURNS, 1)), jnp.arange(TEXT), side="right").astype(jnp.int32),
        "tile_turn": draw_tile_turn(jax.random.fold_in(key_list[10], 71), 0),
        "tile_len": draw_tile_len(jax.random.fold_in(key_list[10], 71), 0),
        "grad_out": normal_values(key_list[9], (TEXT, HEADS * HD), 1.0, 6.0, ((0, 64), (1, 8))),
    }


epsilon = 1e-05

def norm_rows(values, gain):
    inverse = lax.rsqrt(lax.optimization_barrier(jnp.mean(values * values, axis=-1, keepdims=True)) + epsilon)
    return (values * inverse * gain, inverse)

def norm_back(values, inverse, gain, upstream):
    scaled = upstream * gain
    return inverse * scaled - values * inverse ** 3 * lax.optimization_barrier(jnp.mean(values * scaled, axis=-1, keepdims=True))

def key_turns(tile_turn, tile_len, slot_count, tile_size):
    position = jnp.arange(slot_count, dtype=jnp.int32)
    which = position // tile_size
    inside = position - which * tile_size
    onehot = which[:, None] == jnp.arange(tile_turn.shape[0], dtype=jnp.int32)[None, :]
    shown = lax.optimization_barrier(jnp.sum(jnp.where(onehot, tile_turn[None, :], 0), axis=1))
    length = lax.optimization_barrier(jnp.sum(jnp.where(onehot, tile_len[None, :], 0), axis=1))
    return jnp.where(inside < length, shown, TURNS)

def reference(query, vision, w_key, w_value, q_gain, k_gain, text_turn, tile_turn, tile_len, grad_out):
    group = HEADS // KV_HEADS
    scale = 1.0 / math.sqrt(HD)
    q_float = query.astype(jnp.float32).reshape(TEXT, HEADS, HD)
    q_normed, q_inverse = norm_rows(q_float, q_gain)
    q_cast = q_normed.astype(jnp.bfloat16)
    k_raw = jnp.dot(vision, w_key, preferred_element_type=jnp.float32).reshape(VIS, KV_HEADS, HD)
    v_raw = jnp.dot(vision, w_value, preferred_element_type=jnp.float32).reshape(VIS, KV_HEADS, HD)
    k_normed, k_inverse = norm_rows(k_raw, k_gain)
    k_cast = k_normed.astype(jnp.bfloat16)
    v_cast = v_raw.astype(jnp.bfloat16)
    allowed = key_turns(tile_turn, tile_len, VIS, TILE_TOK)[None, :] <= text_turn[:, None]
    upstream = grad_out.reshape(TEXT, HEADS, HD)

    def one_head(carry, head):
        key_acc, value_acc = carry
        kv_index = head // group
        q_head = lax.dynamic_index_in_dim(q_cast, head, 1, keepdims=False)
        qf_head = lax.dynamic_index_in_dim(q_float, head, 1, keepdims=False)
        qi_head = lax.dynamic_index_in_dim(q_inverse, head, 1, keepdims=False)
        up_head = lax.dynamic_index_in_dim(upstream, head, 1, keepdims=False)
        k_head = lax.dynamic_index_in_dim(k_cast, kv_index, 1, keepdims=False)
        v_head = lax.dynamic_index_in_dim(v_cast, kv_index, 1, keepdims=False)
        scores = jnp.dot(q_head, k_head.T, preferred_element_type=jnp.float32) * scale
        expo = jnp.where(allowed, jnp.exp(scores), 0.0)
        probs = (expo / lax.optimization_barrier(jnp.sum(expo, axis=1, keepdims=True))).astype(jnp.bfloat16)
        attended_head = jnp.dot(probs, v_head, preferred_element_type=jnp.float32).astype(jnp.bfloat16)
        d_probs = jnp.dot(up_head, v_head.T, preferred_element_type=jnp.float32)
        delta = lax.optimization_barrier(jnp.sum(up_head.astype(jnp.float32) * attended_head.astype(jnp.float32), axis=1, keepdims=True))
        d_scores = (probs.astype(jnp.float32) * (d_probs - delta)).astype(jnp.bfloat16)
        d_query = jnp.dot(d_scores, k_head, preferred_element_type=jnp.float32) * scale
        grad_head = norm_back(qf_head, qi_head, q_gain, d_query).astype(jnp.bfloat16)
        d_key = jnp.dot(d_scores.T, q_head, preferred_element_type=jnp.float32) * scale
        d_value = jnp.dot(probs.T, up_head, preferred_element_type=jnp.float32)
        key_acc = key_acc.at[kv_index].add(d_key)
        value_acc = value_acc.at[kv_index].add(d_value)
        return ((key_acc, value_acc), (attended_head, grad_head))
    zeros = jnp.zeros((KV_HEADS, VIS, HD), jnp.float32)
    (key_acc, value_acc), (att_heads, grad_heads) = lax.scan(one_head, (zeros, zeros), jnp.arange(HEADS, dtype=jnp.int32))
    attended = att_heads.transpose(1, 0, 2).reshape(TEXT, HEADS * HD)
    grad_query = grad_heads.transpose(1, 0, 2).reshape(TEXT, HEADS * HD)
    d_key_raw = norm_back(k_raw, k_inverse, k_gain, key_acc.transpose(1, 0, 2)).astype(jnp.bfloat16).reshape(VIS, KV_HEADS * HD)
    d_value_cast = value_acc.transpose(1, 0, 2).astype(jnp.bfloat16).reshape(VIS, KV_HEADS * HD)
    grad_w_key = jnp.dot(vision.T, d_key_raw, preferred_element_type=jnp.float32)
    grad_w_value = jnp.dot(vision.T, d_value_cast, preferred_element_type=jnp.float32)
    grad_vision = (jnp.dot(d_key_raw, w_key.T, preferred_element_type=jnp.float32) + jnp.dot(d_value_cast, w_value.T, preferred_element_type=jnp.float32)).astype(jnp.bfloat16)
    return (attended, grad_query, grad_vision, grad_w_key, grad_w_value)
```

```python
import functools
import math

import jax
import jax.numpy as jnp
from jax import lax
from jax.experimental import pallas as pl
from jax.experimental.pallas import tpu as pltpu
from jax.sharding import PartitionSpec as P

HD = 128
TILE_TOK = 256
TURNS = 64
EPS = 1e-05

NY, NZ, NC = 4, 8, 2
NHI, NX = 2, 4
SHARD = 16
CHUNK = NZ * SHARD
SLOTS = NC * NY * CHUNK

BF = jnp.bfloat16
F32 = jnp.float32
MESH = pl.DeviceIdType.MESH
SCALE = 1.0 / math.sqrt(HD)
LOG2E = math.log2(math.e)
MASKED = -16384.0
VMEM_LIMIT = 56 * 1024 * 1024

Y_ORDER = (2, 1, 3) if NY == 4 else tuple(range(1, NY))


def place():
    turn = lax.axis_index("turn")
    core = lax.rem(turn, NC)
    z = lax.rem(turn // NC, NZ)
    y = turn // (NC * NZ)
    return y, z, core


def turn_of(y, z, core):
    return (y * NZ + z) * NC + core


def remote(src, dst, send, recv, **where):
    return pltpu.make_async_remote_copy(
        src_ref=src, dst_ref=dst, send_sem=send, recv_sem=recv, device_id=where, device_id_type=MESH
    )


def turn_peers(y, z, core):
    peers = [turn_of(y, z, 1 - core)]
    peers += [turn_of(lax.rem(y + off, NY), z, core) for off in range(1, NY)]
    peers += [turn_of(y, lax.rem(z + off, NZ), core) for off in range(1, NZ)]
    return peers


def scatter_scratch():
    return [
        pltpu.VMEM((2, NY, CHUNK, HD), BF),
        pltpu.VMEM((2, NY, CHUNK, HD), BF),
        pltpu.VMEM((2, NY, CHUNK, HD), BF),
        pltpu.VMEM((2, NZ, SHARD, HD), F32),
        pltpu.VMEM((2, NZ, SHARD, HD), BF),
        pltpu.VMEM((2, NZ, SHARD, HD), BF),
        pltpu.SemaphoreType.DMA((2, 2, NY)),
        pltpu.SemaphoreType.DMA((2, 2, NY)),
        pltpu.SemaphoreType.DMA((2, 2, NZ)),
    ]


def gather_scratch():
    return [
        pltpu.SemaphoreType.DMA((2, 2, NZ)),
        pltpu.SemaphoreType.DMA((2, 2, NY)),
        pltpu.SemaphoreType.DMA((2, 2, NY)),
    ]


class Scatter:
    def __init__(self, refs, source, own):
        (self.from_c, self.to_y, self.from_y, self.total, self.to_z, self.from_z, self.sc, self.sy, self.sz) = refs
        self.source = source
        self.own = own
        self.sends = []

    def start(self, kind, off):
        y, z, core = place()
        yy = lax.rem(y + off, NY)
        copy = remote(
            self.source(kind, yy), self.from_c.at[kind, yy], self.sc.at[0, kind, off], self.sc.at[1, kind, off],
            turn=turn_of(y, z, 1 - core),
        )
        copy.start()
        self.sends.append(copy)

    def over_core(self, kind):
        y, z, core = place()
        for off in Y_ORDER + (0,):
            yy = lax.rem(y + off, NY)
            remote(
                self.source(kind, yy), self.from_c.at[kind, yy], self.sc.at[0, kind, off], self.sc.at[1, kind, off],
                turn=turn_of(y, z, 1 - core),
            ).wait_recv()
            both = self.own(kind, yy).astype(F32) + self.from_c[kind, yy].astype(F32)
            if off == 0:
                self.total[kind] = both.reshape(NZ, SHARD, HD)
                continue
            self.to_y[kind, off] = both.astype(BF)
            copy = remote(
                self.to_y.at[kind, off], self.from_y.at[kind, off], self.sy.at[0, kind, off], self.sy.at[1, kind, off],
                turn=turn_of(yy, z, core),
            )
            copy.start()
            self.sends.append(copy)

    def over_y(self, kind):
        y, z, core = place()
        total = self.total[kind].reshape(CHUNK, HD)
        for off in (1, 3, 2) if NY == 4 else range(1, NY):
            remote(
                self.to_y.at[kind, off], self.from_y.at[kind, off], self.sy.at[0, kind, off], self.sy.at[1, kind, off],
                turn=turn_of(y, z, core),
            ).wait_recv()
            total = total + self.from_y[kind, off].astype(F32)
        total = total.reshape(NZ, SHARD, HD)
        self.total[kind] = total
        self.to_z[kind] = total.astype(BF)
        for off in range(1, NZ):
            zz = lax.rem(z + off, NZ)
            copy = remote(
                self.to_z.at[kind, zz], self.from_z.at[kind, off], self.sz.at[0, kind, off], self.sz.at[1, kind, off],
                turn=turn_of(y, zz, core),
            )
            copy.start()
            self.sends.append(copy)

    def over_z(self, kind):
        y, z, core = place()
        total = self.total[kind, z]
        for off in range(1, NZ):
            remote(
                self.to_z.at[kind, off], self.from_z.at[kind, off], self.sz.at[0, kind, off], self.sz.at[1, kind, off],
                turn=turn_of(y, z, core),
            ).wait_recv()
            total = total + self.from_z[kind, off].astype(F32)
        return total

    def finish(self):
        for copy in self.sends:
            copy.wait_send()


class Gather:
    def __init__(self, refs, full):
        self.sz, self.sy, self.sc = refs
        self.full = full
        self.sends = []

    def go(self, src, sem, **where):
        copy = remote(src, src, sem[0], sem[1], **where)
        copy.start()
        self.sends.append(copy)

    def arrived(self, dst, sem):
        y, z, core = place()
        remote(dst, dst, sem[0], sem[1], turn=turn_of(y, z, 1 - core)).wait_recv()

    def over_z(self, kind, shard):
        y, z, core = place()
        self.full[kind, core, y, z] = shard.astype(BF)
        for off in range(1, NZ):
            self.go(
                self.full.at[kind, core, y, z], (self.sz.at[0, kind, off], self.sz.at[1, kind, off]),
                turn=turn_of(y, lax.rem(z + off, NZ), core),
            )

    def over_y(self, kind):
        y, z, core = place()
        for off in range(1, NZ):
            self.arrived(
                self.full.at[kind, core, y, lax.rem(z + NZ - off, NZ)], (self.sz.at[0, kind, off], self.sz.at[1, kind, off])
            )
        for off in Y_ORDER:
            self.go(
                self.full.at[kind, core, y], (self.sy.at[0, kind, off], self.sy.at[1, kind, off]),
                turn=turn_of(lax.rem(y + off, NY), z, core),
            )
        self.go(
            self.full.at[kind, core, y], (self.sc.at[0, kind, 0], self.sc.at[1, kind, 0]), turn=turn_of(y, z, 1 - core)
        )

    def over_core(self, kind, off):
        y, z, core = place()
        chunk = self.full.at[kind, core, lax.rem(y + NY - off, NY)]
        self.arrived(chunk, (self.sy.at[0, kind, off], self.sy.at[1, kind, off]))
        self.go(chunk, (self.sc.at[0, kind, off], self.sc.at[1, kind, off]), turn=turn_of(y, z, 1 - core))

    def last(self, kind, off):
        y, z, core = place()
        chunk = self.full.at[kind, 1 - core, lax.rem(y + NY - off, NY)]
        self.arrived(chunk, (self.sc.at[0, kind, off], self.sc.at[1, kind, off]))

    def finish(self):
        for copy in self.sends:
            copy.wait_send()


def inverse_rms(values):
    return lax.rsqrt(jnp.mean(values * values, axis=-1, keepdims=True) + EPS)


def project_kernel(vision, w_key, w_value, k_gain, full, raw, to_c, own, *scratch):
    y, z, core = place()
    barrier = pltpu.get_barrier_semaphore()
    peers = turn_peers(y, z, core)
    for peer in peers:
        pl.semaphore_signal(barrier, inc=1, device_id={"turn": peer}, device_id_type=MESH)

    def partial(kind, cc, yy):
        weight = (w_key, w_value)[kind]
        return jnp.dot(vision[cc, yy], weight[...], preferred_element_type=F32)

    scatter = Scatter(scratch[:9], lambda kind, yy: to_c.at[kind, yy], lambda kind, yy: own[kind, yy])
    gather = Gather(scratch[9:], full)
    for kind in range(2):
        for off in range(NY):
            yy = lax.rem(y + off, NY)
            to_c[kind, yy] = partial(kind, 1 - core, yy).astype(BF)
    pl.semaphore_wait(barrier, len(peers))
    for kind in range(2):
        for off in Y_ORDER + (0,):
            scatter.start(kind, off)
    for kind in range(2):
        for off in range(NY):
            yy = lax.rem(y + off, NY)
            own[kind, yy] = partial(kind, core, yy)
    for kind in range(2):
        scatter.over_core(kind)
    for kind in range(2):
        scatter.over_y(kind)
    for kind in range(2):
        total = scatter.over_z(kind)
        if kind == 0:
            raw[...] = total
            total = total * inverse_rms(total) * k_gain[...]
        gather.over_z(kind, total)
    for kind in range(2):
        gather.over_y(kind)
    for off in (1, 3, 2) if NY == 4 else range(1, NY):
        for kind in range(2):
            gather.over_core(kind, off)
    for off in range(NY):
        for kind in range(2):
            gather.last(kind, off)
    scatter.finish()
    gather.finish()


def project(vision, w_key, w_value, k_gain):
    vmem = pl.BlockSpec(memory_space=pltpu.VMEM)
    return pl.pallas_call(
        project_kernel,
        out_shape=(
            jax.ShapeDtypeStruct((2, NC, NY, NZ, SHARD, HD), BF),
            jax.ShapeDtypeStruct((SHARD, HD), F32),
        ),
        in_specs=[vmem] * 4,
        out_specs=(vmem, vmem),
        scratch_shapes=[
            pltpu.VMEM((2, NY, CHUNK, HD), BF),
            pltpu.VMEM((2, NY, CHUNK, HD), F32),
        ]
        + scatter_scratch()
        + gather_scratch(),
        compiler_params=pltpu.CompilerParams(collective_id=0, has_side_effects=True, vmem_limit_bytes=VMEM_LIMIT),
        name="project",
    )(vision.reshape(NC, NY, CHUNK, vision.shape[1]), w_key, w_value, k_gain)


def attend_kernel(tile_turn, tile_len, query, grad_out, kv, text_turn, q_gain, attended, grad_query, d_kv, qa, ka, va, da, acc):
    step = pl.program_id(0)
    rows = query.shape[0]

    @pl.when(step == 0)
    def _():
        ka[:, :HD] = kv[0]
        va[:, :HD] = kv[1]
        va[:, HD:] = jnp.ones((SLOTS, HD), BF)
        for tile in range(SLOTS // TILE_TOK):
            inside = lax.broadcasted_iota(jnp.int32, (TILE_TOK, HD), 0)
            turn = lax.broadcasted_iota(jnp.int32, (TILE_TOK, HD), 1)
            shown = jnp.where(inside < tile_len[tile], tile_turn[tile], TURNS)
            hidden = jnp.logical_and(shown > turn, turn < TURNS)
            ka[pl.ds(tile * TILE_TOK, TILE_TOK), HD:] = jnp.where(hidden, MASKED, 0.0).astype(BF)
        turn = lax.broadcasted_iota(jnp.int32, (rows, HD), 1)
        qa[:, HD:] = jnp.where(text_turn[...] == turn, 1.0, 0.0).astype(BF)
        acc[...] = jnp.zeros_like(acc)

    gain = q_gain[...]
    q_float = query[...].astype(F32)
    inverse = inverse_rms(q_float)
    qa[:, :HD] = (q_float * inverse * gain * (SCALE * LOG2E)).astype(BF)
    scores = lax.dot_general(qa[...], ka[...], (((1,), (1,)), ((), ())), preferred_element_type=F32)
    expo = jnp.exp2(scores).astype(BF)
    summed = jnp.dot(expo, va[...], preferred_element_type=F32)
    over = 1.0 / summed[:, HD:]
    att = (summed[:, :HD] * over).astype(BF)
    attended[...] = att
    up = grad_out[...].astype(F32)
    delta = -jnp.sum(up * att.astype(F32), axis=1, keepdims=True) * over
    high = delta.astype(BF)
    low = (delta - high.astype(F32)).astype(BF)
    lane = lax.broadcasted_iota(jnp.int32, (rows, HD), 1)
    da[:, :HD] = (up * over).astype(BF)
    da[:, HD:] = jnp.where(lane == 0, high, jnp.where(lane == 1, low, jnp.zeros_like(low)))
    d_probs = lax.dot_general(da[...], va[...], (((1,), (1,)), ((), ())), preferred_element_type=F32)
    d_scores = expo * d_probs.astype(BF)
    d_query = jnp.dot(d_scores, ka[:, :HD], preferred_element_type=F32)
    scaled = d_query * (gain * SCALE)
    grad_query[...] = (
        inverse * scaled - q_float * (inverse * inverse * inverse) * jnp.mean(q_float * scaled, axis=1, keepdims=True)
    ).astype(BF)
    acc[0] += lax.dot_general(d_scores, qa[:, :HD], (((0,), (0,)), ((), ())), preferred_element_type=F32)
    acc[1] += lax.dot_general(expo, da[:, :HD], (((0,), (0,)), ((), ())), preferred_element_type=F32)

    @pl.when(step == pl.num_programs(0) - 1)
    def _():
        d_kv[0] = (acc[0] * (1.0 / LOG2E)).astype(BF)
        d_kv[1] = acc[1].astype(BF)


def attend(query, grad_out, kv, text_turn, tile_turn, tile_len, q_gain):
    rows, width = query.shape
    heads = width // HD
    smem = pl.BlockSpec(memory_space=pltpu.SMEM)
    block = pl.BlockSpec((rows, HD), lambda h: (0, h))

    def whole(*shape):
        return pl.BlockSpec(shape, lambda h: (0,) * len(shape))

    return pl.pallas_call(
        attend_kernel,
        grid=(heads,),
        out_shape=(
            jax.ShapeDtypeStruct(query.shape, BF),
            jax.ShapeDtypeStruct(query.shape, BF),
            jax.ShapeDtypeStruct((2, SLOTS, HD), BF),
        ),
        in_specs=[smem, smem, block, block, whole(2, SLOTS, HD), whole(rows, 1), whole(1, HD)],
        out_specs=(block, block, whole(2, SLOTS, HD)),
        scratch_shapes=[
            pltpu.VMEM((rows, 2 * HD), BF),
            pltpu.VMEM((SLOTS, 2 * HD), BF),
            pltpu.VMEM((SLOTS, 2 * HD), BF),
            pltpu.VMEM((rows, 2 * HD), BF),
            pltpu.VMEM((2, SLOTS, HD), F32),
        ],
        compiler_params=pltpu.CompilerParams(vmem_limit_bytes=VMEM_LIMIT),
        name="attend",
    )(tile_turn, tile_len, query, grad_out, kv, text_turn, q_gain)


def finish_kernel(
    d_kv, vision, w_key, w_value, raw, k_gain, grad_vision, grad_w_key, grad_w_value, full, to_x, from_x, to_hi, from_hi, sx, rx, sh, *scratch
):
    y, z, core = place()
    head = lax.axis_index("head")
    hi, x = head // NX, lax.rem(head, NX)
    barrier = pltpu.get_barrier_semaphore()
    peers = turn_peers(y, z, core)
    heads = [hi * NX + lax.rem(x + off, NX) for off in range(1, NX)] + [(1 - hi) * NX + x]
    for peer in peers:
        pl.semaphore_signal(barrier, inc=1, device_id={"turn": peer}, device_id_type=MESH)
    for peer in heads:
        pl.semaphore_signal(barrier, inc=1, device_id={"head": peer}, device_id_type=MESH)
    pl.semaphore_wait(barrier, len(peers) + len(heads))

    scatter = Scatter(
        scratch[:9], lambda kind, yy: d_kv.at[kind, 1 - core, yy], lambda kind, yy: d_kv[kind, core, yy]
    )
    gather = Gather(scratch[9:], full)
    for kind in range(2):
        for off in Y_ORDER + (0,):
            scatter.start(kind, off)
    for kind in range(2):
        scatter.over_core(kind)
    for kind in range(2):
        scatter.over_y(kind)
    for kind in range(2):
        total = scatter.over_z(kind)
        if kind == 0:
            raw_values = raw[...]
            inverse = inverse_rms(raw_values)
            scaled = total * k_gain[...]
            total = inverse * scaled - raw_values * (inverse * inverse * inverse) * jnp.mean(
                raw_values * scaled, axis=1, keepdims=True
            )
        gather.over_z(kind, total)
    for kind in range(2):
        gather.over_y(kind)

    def to_head(which, cc, off, yy):
        slot = lax.rem(yy - x + NX + NX - 1, NX)
        return remote(
            to_x.at[which, off], from_x.at[cc, slot], sx.at[which, off], rx.at[cc, slot], head=hi * NX + yy
        )

    def vision_term(which, off):
        cc = core if which == 0 else 1 - core
        yy = lax.rem(y + NY - off, NY)
        term = lax.dot_general(
            full[0, cc, yy].reshape(CHUNK, HD), w_key[...], (((1,), (1,)), ((), ())), preferred_element_type=F32
        ) + lax.dot_general(
            full[1, cc, yy].reshape(CHUNK, HD), w_value[...], (((1,), (1,)), ((), ())), preferred_element_type=F32
        )
        to_x[which, off] = term.astype(BF)

        @pl.when(yy != x)
        def _():
            to_head(which, cc, off, yy).start()

    vision_term(0, 0)
    order = (1, 3, 2) if NY == 4 else tuple(range(1, NY))
    for off in order:
        for kind in range(2):
            gather.over_core(kind, off)
        vision_term(0, off)
    for off in (0,) + order:
        for kind in range(2):
            gather.last(kind, off)
        vision_term(1, off)

    def summed(cc):
        total = to_x[lax.rem(cc + core, NC), lax.rem(y - x + NY, NY)].astype(F32)
        for slot in range(NX - 1):
            remote(from_x.at[cc, slot], from_x.at[cc, slot], sx.at[0, slot], rx.at[cc, slot], head=heads[0]).wait_recv()
            total = total + from_x[cc, slot].astype(F32)
        return total

    to_hi[...] = summed(1 - hi).astype(BF)
    over_hi = remote(to_hi, from_hi, sh.at[0], sh.at[1], head=(1 - hi) * NX + x)
    over_hi.start()
    kept = summed(hi)
    for kind, out in ((0, grad_w_key), (1, grad_w_value)):
        out[...] = lax.dot_general(
            vision[...], full[kind].reshape(SLOTS, HD), (((0,), (0,)), ((), ())), preferred_element_type=F32
        )
    over_hi.wait_recv()
    grad_vision[...] = (kept + from_hi[...].astype(F32)).astype(BF)
    over_hi.wait_send()
    for which in range(2):
        cc = core if which == 0 else 1 - core
        for off in range(NY):
            yy = lax.rem(y + NY - off, NY)

            @pl.when(yy != x)
            def _(which=which, cc=cc, off=off, yy=yy):
                to_head(which, cc, off, yy).wait_send()

    scatter.finish()
    gather.finish()


def finish(d_kv, vision, w_key, w_value, raw, k_gain):
    vmem = pl.BlockSpec(memory_space=pltpu.VMEM)
    width = vision.shape[1]
    return pl.pallas_call(
        finish_kernel,
        out_shape=(
            jax.ShapeDtypeStruct((CHUNK, width), BF),
            jax.ShapeDtypeStruct((width, HD), F32),
            jax.ShapeDtypeStruct((width, HD), F32),
        ),
        in_specs=[vmem] * 6,
        out_specs=(vmem,) * 3,
        scratch_shapes=[
            pltpu.VMEM((2, NC, NY, NZ, SHARD, HD), BF),
            pltpu.VMEM((2, NY, CHUNK, width), BF),
            pltpu.VMEM((2, NX, CHUNK, width), BF),
            pltpu.VMEM((CHUNK, width), BF),
            pltpu.VMEM((CHUNK, width), BF),
            pltpu.SemaphoreType.DMA((2, NY)),
            pltpu.SemaphoreType.DMA((2, NX)),
            pltpu.SemaphoreType.DMA((2,)),
        ]
        + scatter_scratch()
        + gather_scratch(),
        compiler_params=pltpu.CompilerParams(collective_id=1, has_side_effects=True, vmem_limit_bytes=VMEM_LIMIT),
        name="finish",
    )(d_kv.reshape(2, NC, NY, CHUNK, HD), vision, w_key, w_value, raw, k_gain)


def body(query, vision, w_key, w_value, q_gain, k_gain, text_turn, tile_turn, tile_len, grad_out):
    k_gain = k_gain.reshape(1, HD)
    full, raw = project(vision, w_key, w_value, k_gain)
    attended, grad_query, d_kv = attend(
        query, grad_out, full.reshape(2, SLOTS, HD), text_turn.reshape(-1, 1), tile_turn, tile_len, q_gain.reshape(1, HD)
    )
    grad_vision, grad_w_key, grad_w_value = finish(d_kv, vision, w_key, w_value, raw, k_gain)
    return (attended, grad_query, grad_vision, grad_w_key, grad_w_value)


def solution(mesh):
    return jax.shard_map(
        body,
        mesh=mesh,
        in_specs=(
            P("turn", "head"),
            P(None, "turn"),
            P("turn", "head"),
            P("turn", "head"),
            P(),
            P(),
            P("turn"),
            P(),
            P(),
            P("turn", "head"),
        ),
        out_specs=(
            P("turn", "head"),
            P("turn", "head"),
            P("head", "turn"),
            P("turn", "head"),
            P("turn", "head"),
        ),
        check_vma=False,
    )
```

```python
import math

import jax
import jax.numpy as jnp
from jax import lax
from jax.experimental import pallas as pl
from jax.experimental.pallas import tpu as pltpu
from jax.sharding import PartitionSpec as P

HD = 128
TILE_TOK = 256
TURNS = 64
EPS = 1e-05

NY, NZ, NC = 4, 8, 2
NHI, NX = 2, 4
CHUNK = 128
OWN_LO, OWNERS = 3, 2
SHARD = CHUNK // OWNERS
SLOTS = NC * NY * CHUNK

BF = jnp.bfloat16
F32 = jnp.float32
MESH = pl.DeviceIdType.MESH
SCALE = 1.0 / math.sqrt(HD)
LOG2E = math.log2(math.e)
MASKED = -16384.0
VMEM_LIMIT = 56 * 1024 * 1024

Y_ORDER = (2, 1, 3)
Y_ARRIVAL = (1, 3, 2)


def place():
    turn = lax.axis_index("turn")
    core = lax.rem(turn, NC)
    z = lax.rem(turn // NC, NZ)
    y = turn // (NC * NZ)
    return y, z, core


def turn_of(y, z, core):
    return (y * NZ + z) * NC + core


def is_owner(z):
    return jnp.logical_and(z >= OWN_LO, z < OWN_LO + OWNERS)


def remote(src, dst, send, recv, **where):
    return pltpu.make_async_remote_copy(
        src_ref=src, dst_ref=dst, send_sem=send, recv_sem=recv, device_id=where, device_id_type=MESH
    )


def scatter_scratch():
    return [
        pltpu.VMEM((2, NY, CHUNK, HD), BF),
        pltpu.VMEM((2, NY, CHUNK, HD), BF),
        pltpu.VMEM((2, NY, CHUNK, HD), BF),
        pltpu.VMEM((2, OWNERS, SHARD, HD), F32),
        pltpu.VMEM((2, OWNERS, SHARD, HD), BF),
        pltpu.VMEM((2, NZ, SHARD, HD), BF),
        pltpu.SemaphoreType.DMA((2, 2, NY)),
        pltpu.SemaphoreType.DMA((2, 2, NY)),
        pltpu.SemaphoreType.DMA((2, 2, NZ)),
    ]


def gather_scratch():
    return [
        pltpu.VMEM((2, NC, NY, OWNERS, SHARD, HD), BF),
        pltpu.SemaphoreType.DMA((2, 2, NZ)),
        pltpu.SemaphoreType.DMA((2, 2, NY)),
        pltpu.SemaphoreType.DMA((2, 2, NY)),
    ]


class Scatter:
    def __init__(self, refs, source, own):
        (self.from_c, self.to_y, self.from_y, self.total, self.to_z, self.from_z, self.sc, self.sy, self.sz) = refs
        self.source = source
        self.own = own

    def core_copy(self, kind, off):
        y, z, core = place()
        yy = lax.rem(y + off, NY)
        return remote(
            self.source(kind, yy), self.from_c.at[kind, yy], self.sc.at[0, kind, off], self.sc.at[1, kind, off],
            turn=turn_of(y, z, 1 - core),
        )

    def y_copy(self, kind, off):
        y, z, core = place()
        return remote(
            self.to_y.at[kind, off], self.from_y.at[kind, off], self.sy.at[0, kind, off], self.sy.at[1, kind, off],
            turn=turn_of(lax.rem(y + off, NY), z, core),
        )

    def z_copy(self, kind, step):
        y, z, core = place()
        far = z // (NZ // 2)
        owner = (OWNERS - 1 - step) * (1 - far) + step * far
        copy = remote(
            self.to_z.at[kind, owner], self.from_z.at[kind, z], self.sz.at[0, kind, owner], self.sz.at[1, kind, z],
            turn=turn_of(y, owner + OWN_LO, core),
        )
        return owner + OWN_LO != z, copy

    def start(self, kind):
        for off in Y_ORDER + (0,):
            self.core_copy(kind, off).start()

    def over_core(self, kind):
        y, z, core = place()
        for off in Y_ORDER + (0,):
            yy = lax.rem(y + off, NY)
            self.core_copy(kind, off).wait_recv()
            both = self.own(kind, yy).astype(F32) + self.from_c[kind, yy].astype(F32)
            if off == 0:
                self.total[kind] = both.reshape(OWNERS, SHARD, HD)
            else:
                self.to_y[kind, off] = both.astype(BF)
                self.y_copy(kind, off).start()

    def over_y(self, kind):
        total = self.total[kind].reshape(CHUNK, HD)
        for off in Y_ARRIVAL:
            self.y_copy(kind, off).wait_recv()
            total = total + self.from_y[kind, off].astype(F32)
        total = total.reshape(OWNERS, SHARD, HD)
        self.total[kind] = total
        self.to_z[kind] = total.astype(BF)
        for step in range(OWNERS):
            other, copy = self.z_copy(kind, step)

            @pl.when(other)
            def _(copy=copy):
                copy.start()

    def over_z(self, kind, then):
        y, z, core = place()

        @pl.when(is_owner(z))
        def _():
            total = self.total[kind, z - OWN_LO]
            for off in (1, 7, 2, 6, 3, 5, 4):
                zz = lax.rem(z + off, NZ)
                remote(
                    self.to_z.at[kind, 0], self.from_z.at[kind, zz], self.sz.at[0, kind, 0], self.sz.at[1, kind, zz],
                    turn=turn_of(y, zz, core),
                ).wait_recv()
                total = total + self.from_z[kind, zz].astype(F32)
            then(total)

    def finish(self):
        for kind in range(2):
            for off in range(NY):
                self.core_copy(kind, off).wait_send()
            for off in range(1, NY):
                self.y_copy(kind, off).wait_send()
            for step in range(OWNERS):
                other, copy = self.z_copy(kind, step)

                @pl.when(other)
                def _(copy=copy):
                    copy.wait_send()


class Gather:
    def __init__(self, refs):
        self.full, self.sz, self.sy, self.sc = refs

    def z_copy(self, kind, off):
        y, z, core = place()
        src = self.full.at[kind, core, y, z - OWN_LO]
        return remote(
            src, src, self.sz.at[0, kind, off], self.sz.at[1, kind, z - OWN_LO], turn=turn_of(y, lax.rem(z + off, NZ), core)
        )

    def y_copy(self, kind, off):
        y, z, core = place()
        src = self.full.at[kind, core, y]
        return remote(
            src, src, self.sy.at[0, kind, off], self.sy.at[1, kind, off], turn=turn_of(lax.rem(y + off, NY), z, core)
        )

    def core_copy(self, kind, off):
        y, z, core = place()
        src = self.full.at[kind, core, lax.rem(y + NY - off, NY)]
        return remote(src, src, self.sc.at[0, kind, off], self.sc.at[1, kind, off], turn=turn_of(y, z, 1 - core))

    def arrived(self, dst, sem):
        y, z, core = place()
        remote(dst, dst, sem[0], sem[1], turn=turn_of(y, z, 1 - core)).wait_recv()

    def over_z(self, kind, shard):
        y, z, core = place()
        self.full[kind, core, y, z - OWN_LO] = shard.astype(BF)
        for off in (4, 3, 5, 2, 6, 1, 7):
            self.z_copy(kind, off).start()

    def over_y(self, kind):
        y, z, core = place()
        for owner in range(OWNERS):

            @pl.when(z != owner + OWN_LO)
            def _(owner=owner):
                self.arrived(self.full.at[kind, core, y, owner], (self.sz.at[0, kind, 0], self.sz.at[1, kind, owner]))

        for off in Y_ORDER:
            self.y_copy(kind, off).start()
        self.core_copy(kind, 0).start()

    def over_core(self, kind, off):
        y, z, core = place()
        self.arrived(
            self.full.at[kind, core, lax.rem(y + NY - off, NY)], (self.sy.at[0, kind, off], self.sy.at[1, kind, off])
        )
        self.core_copy(kind, off).start()

    def last(self, kind, off):
        y, z, core = place()
        self.arrived(
            self.full.at[kind, 1 - core, lax.rem(y + NY - off, NY)], (self.sc.at[0, kind, off], self.sc.at[1, kind, off])
        )

    def finish(self):
        y, z, core = place()
        for kind in range(2):
            for off in range(1, NY):
                self.y_copy(kind, off).wait_send()
            for off in range(NY):
                self.core_copy(kind, off).wait_send()

            @pl.when(is_owner(z))
            def _(kind=kind):
                for off in range(1, NZ):
                    self.z_copy(kind, off).wait_send()


def inverse_rms(values):
    return lax.rsqrt(jnp.mean(values * values, axis=-1, keepdims=True) + EPS)


def rows_dot(a, b):
    return lax.dot_general(a, b, (((1,), (1,)), ((), ())), preferred_element_type=F32)


def columns_dot(a, b):
    return lax.dot_general(a, b, (((0,), (0,)), ((), ())), preferred_element_type=F32)


def cross_kernel(
    tile_turn, tile_len, query, grad_out, vision, w_key, w_value, text_turn, q_gain, k_gain,
    attended, grad_query, grad_vision, grad_w_key, grad_w_value,
    q_buf, up_buf, att_buf, gq_buf, s_in, s_out, qa, da, ka, va, inv, expo, slot_grad,
    to_c, own, raw, d_kv, to_x, from_x, to_hi, from_hi, sx, rx, sh, *scratch
):
    y, z, core = place()
    head = lax.axis_index("head")
    hi, x = head // NX, lax.rem(head, NX)
    heads, rows = q_buf.shape[0], q_buf.shape[1]

    barrier = pltpu.get_barrier_semaphore()

    def greet(**peer):
        pl.semaphore_signal(barrier, inc=1, device_id=peer, device_id_type=MESH)

    x_peers = [hi * NX + lax.rem(x + off, NX) for off in range(1, NX)]
    greet(head=(1 - hi) * NX + x)

    @pl.when(is_owner(z))
    def _():
        for off in range(1, NZ):
            greet(turn=turn_of(y, lax.rem(z + off, NZ), core))

    @pl.when(jnp.logical_not(is_owner(z)))
    def _():
        for owner in range(OWNERS):
            greet(turn=turn_of(y, owner + OWN_LO, core))

    for off in range(1, NY):
        greet(turn=turn_of(lax.rem(y + off, NY), z, core))
    for peer in x_peers:
        greet(head=peer)
    greet(turn=turn_of(y, z, 1 - core))

    def load(h, which):
        src, dst = ((query, q_buf), (grad_out, up_buf))[which]
        return pltpu.make_async_copy(src.at[:, pl.ds(h * HD, HD)], dst.at[h], s_in.at[which, h])

    def save(h, which):
        src, dst = ((att_buf, attended), (gq_buf, grad_query))[which]
        start = h * HD if isinstance(h, int) else pl.multiple_of(h * HD, HD)
        return pltpu.make_async_copy(src.at[h], dst.at[:, pl.ds(start, HD)], s_out.at[which, h])

    for which in range(2):
        for h in range(heads):
            load(h, which).start()

    def partial(kind, cc, yy):
        weight = (w_key, w_value)[kind]
        return jnp.dot(vision[cc, yy], weight[...], preferred_element_type=F32)

    for kind in range(2):
        for yy in range(NY):
            to_c[kind, yy] = partial(kind, 1 - core, yy).astype(BF)
            own[kind, yy] = partial(kind, core, yy)

    for tile in range(SLOTS // TILE_TOK):
        inside = lax.broadcasted_iota(jnp.int32, (TILE_TOK, HD), 0)
        turn = lax.broadcasted_iota(jnp.int32, (TILE_TOK, HD), 1)
        shown = jnp.where(inside < tile_len[tile], tile_turn[tile], TURNS)
        hidden = jnp.logical_and(shown > turn, turn < TURNS)
        ka[pl.ds(tile * TILE_TOK, TILE_TOK), HD:] = jnp.where(hidden, MASKED, 0.0).astype(BF)
    va[:, HD:] = jnp.ones((SLOTS, HD), BF)
    for part in range(rows // HD):
        turn = lax.broadcasted_iota(jnp.int32, (HD, HD), 0)
        chosen = jnp.where(turn == text_turn[pl.ds(part, 1), :], 1.0, 0.0).T.astype(BF)
        for h in range(heads):
            qa[h, pl.ds(part * HD, HD), HD:] = chosen

    gain_q = q_gain[...]

    def norm_queries(h, carry):
        q_float = q_buf[h].astype(F32)
        inverse = inverse_rms(q_float)
        inv[h] = inverse
        qa[h, :, :HD] = (q_float * inverse * (gain_q * (SCALE * LOG2E))).astype(BF)
        return carry

    for which in range(2):
        for h in range(heads):
            load(h, which).wait()
    lax.fori_loop(0, heads, norm_queries, 0)

    common = NY + NX
    @pl.when(is_owner(z))
    def _():
        pl.semaphore_wait(barrier, common + NZ - 1)

    @pl.when(jnp.logical_not(is_owner(z)))
    def _():
        pl.semaphore_wait(barrier, common + OWNERS)

    scatter = Scatter(scratch[:9], lambda kind, yy: to_c.at[kind, yy], lambda kind, yy: own[kind, yy])
    gather = Gather(scratch[9:13])
    for kind in range(2):
        scatter.start(kind)
    for kind in range(2):
        scatter.over_core(kind)
    for kind in range(2):
        scatter.over_y(kind)

    def key_shard(total):
        raw[...] = total
        gather.over_z(0, total * inverse_rms(total) * k_gain[...])

    scatter.over_z(0, key_shard)
    scatter.over_z(1, lambda total: gather.over_z(1, total))
    for kind in range(2):
        gather.over_y(kind)
    for off in Y_ARRIVAL:
        for kind in range(2):
            gather.over_core(kind, off)
    for off in range(NY):
        for kind in range(2):
            gather.last(kind, off)
    ka[:, :HD] = gather.full[0].reshape(SLOTS, HD)
    va[:, :HD] = gather.full[1].reshape(SLOTS, HD)

    lane = lax.broadcasted_iota(jnp.int32, (rows, HD), 1)
    slot_grad[...] = jnp.zeros_like(slot_grad)

    def forward(h):
        weights = jnp.exp2(rows_dot(qa[h], ka[...])).astype(BF)
        expo[h] = weights
        summed = jnp.dot(weights, va[...], preferred_element_type=F32)
        over = 1.0 / summed[:, HD:]
        att = (summed[:, :HD] * over).astype(BF)
        att_buf[h] = att
        save(h, 0).start()
        up = up_buf[h].astype(F32)
        delta = -jnp.sum(up * att.astype(F32), axis=1, keepdims=True) * over
        high = delta.astype(BF)
        low = (delta - high.astype(F32)).astype(BF)
        up = (up * over).astype(BF)
        da[h, :, :HD] = up
        da[h, :, HD:] = jnp.where(lane == 0, high, jnp.where(lane == 1, low, jnp.zeros_like(low)))
        slot_grad[1] += columns_dot(up, weights)

    def forward_pair(pair, carry):
        forward(2 * pair)
        forward(2 * pair + 1)
        return carry

    lax.fori_loop(0, heads // 2, forward_pair, 0)

    sums = Scatter(
        scratch[13:22], lambda kind, yy: d_kv.at[kind, 1 - core, yy], lambda kind, yy: d_kv[kind, core, yy]
    )
    back = Gather(scratch[22:26])

    def put(kind, factor):
        for cc in range(NC):
            for yy in range(NY):
                d_kv[kind, cc, yy] = (slot_grad[kind, :, pl.ds((cc * NY + yy) * CHUNK, CHUNK)] * factor).T.astype(BF)

    put(1, 1.0)
    sums.start(1)

    def backward(h):
        d_scores = expo[h] * rows_dot(da[h], va[...]).astype(BF)
        expo[h] = d_scores
        slot_grad[0] += columns_dot(qa[h, :, :HD], d_scores)

    def backward_pair(pair, carry):
        backward(2 * pair)
        backward(2 * pair + 1)

        @pl.when(pair == 0)
        def _():
            sums.over_core(1)

        @pl.when(pair == 3)
        def _():
            sums.over_y(1)

        return carry

    lax.fori_loop(0, heads // 2, backward_pair, 0)
    put(0, 1.0 / LOG2E)
    sums.start(0)

    def query_grad(h):
        d_query = jnp.dot(expo[h], ka[:, :HD], preferred_element_type=F32)
        q_float = q_buf[h].astype(F32)
        inverse = inv[h]
        scaled = d_query * (gain_q * SCALE)
        gq_buf[h] = (
            inverse * scaled - q_float * (inverse * inverse * inverse) * jnp.mean(q_float * scaled, axis=1, keepdims=True)
        ).astype(BF)
        save(h, 1).start()

    def query_pair(pair, carry):
        query_grad(2 * pair)
        query_grad(2 * pair + 1)

        @pl.when(pair == 0)
        def _():
            sums.over_core(0)

        @pl.when(pair == 3)
        def _():
            sums.over_y(0)

        return carry

    lax.fori_loop(0, heads // 2, query_pair, 0)

    sums.over_z(1, lambda total: back.over_z(1, total))

    def key_grad_shard(total):
        raw_values = raw[...]
        inverse = inverse_rms(raw_values)
        scaled = total * k_gain[...]
        back.over_z(
            0,
            inverse * scaled
            - raw_values * (inverse * inverse * inverse) * jnp.mean(raw_values * scaled, axis=1, keepdims=True),
        )

    sums.over_z(0, key_grad_shard)
    back.over_y(1)
    back.over_y(0)

    full = back.full

    def to_head(which, off):
        y, z, core = place()
        cc = core if which == 0 else 1 - core
        yy = lax.rem(y + NY - off, NY)
        slot = lax.rem(yy - x + NX + NX - 1, NX)
        return yy != x, remote(
            to_x.at[which, off], from_x.at[cc, slot], sx.at[which, off], rx.at[cc, slot], head=hi * NX + yy
        )

    def vision_term(which, off):
        cc = core if which == 0 else 1 - core
        yy = lax.rem(y + NY - off, NY)
        term = rows_dot(full[0, cc, yy].reshape(CHUNK, HD), w_key[...]) + rows_dot(
            full[1, cc, yy].reshape(CHUNK, HD), w_value[...]
        )
        to_x[which, off] = term.astype(BF)
        other, copy = to_head(which, off)

        @pl.when(other)
        def _():
            copy.start()

    vision_term(0, 0)
    for off in Y_ARRIVAL:
        for kind in (1, 0):
            back.over_core(kind, off)
        vision_term(0, off)
    for off in (0,) + Y_ARRIVAL:
        for kind in (1, 0):
            back.last(kind, off)
        vision_term(1, off)

    def summed_over_x(cc):
        total = to_x[lax.rem(cc + core, NC), lax.rem(y - x + NY, NY)].astype(F32)
        for slot in range(NX - 1):
            remote(
                from_x.at[cc, slot], from_x.at[cc, slot], sx.at[0, slot], rx.at[cc, slot], head=x_peers[0]
            ).wait_recv()
            total = total + from_x[cc, slot].astype(F32)
        return total

    to_hi[...] = summed_over_x(1 - hi).astype(BF)
    over_hi = remote(to_hi, from_hi, sh.at[0], sh.at[1], head=(1 - hi) * NX + x)
    over_hi.start()
    kept = summed_over_x(hi)
    for kind, out in ((0, grad_w_key), (1, grad_w_value)):
        out[...] = columns_dot(vision[...].reshape(SLOTS, vision.shape[-1]), full[kind].reshape(SLOTS, HD))
    scatter.finish()
    gather.finish()
    sums.finish()
    back.finish()
    for which in range(2):
        for h in range(heads):
            save(h, which).wait()
        for off in range(NY):
            other, copy = to_head(which, off)

            @pl.when(other)
            def _(copy=copy):
                copy.wait_send()

    over_hi.wait_recv()
    grad_vision[...] = (kept + from_hi[...].astype(F32)).astype(BF)
    over_hi.wait_send()


def cross(tile_turn, tile_len, query, grad_out, vision, w_key, w_value, text_turn, q_gain, k_gain):
    vmem = pl.BlockSpec(memory_space=pltpu.VMEM)
    smem = pl.BlockSpec(memory_space=pltpu.SMEM)
    hbm = pl.BlockSpec(memory_space=pl.ANY)
    rows, columns = query.shape
    heads = columns // HD
    width = vision.shape[1]
    return pl.pallas_call(
        cross_kernel,
        out_shape=(
            jax.ShapeDtypeStruct(query.shape, BF),
            jax.ShapeDtypeStruct(query.shape, BF),
            jax.ShapeDtypeStruct((CHUNK, width), BF),
            jax.ShapeDtypeStruct((width, HD), F32),
            jax.ShapeDtypeStruct((width, HD), F32),
        ),
        in_specs=[smem, smem, hbm, hbm] + [vmem] * 6,
        out_specs=(hbm, hbm) + (vmem,) * 3,
        scratch_shapes=[
            pltpu.VMEM((heads, rows, HD), BF),
            pltpu.VMEM((heads, rows, HD), BF),
            pltpu.VMEM((heads, rows, HD), BF),
            pltpu.VMEM((heads, rows, HD), BF),
            pltpu.SemaphoreType.DMA((2, heads)),
            pltpu.SemaphoreType.DMA((2, heads)),
            pltpu.VMEM((heads, rows, 2 * HD), BF),
            pltpu.VMEM((heads, rows, 2 * HD), BF),
            pltpu.VMEM((SLOTS, 2 * HD), BF),
            pltpu.VMEM((SLOTS, 2 * HD), BF),
            pltpu.VMEM((heads, rows, 1), F32),
            pltpu.VMEM((heads, rows, SLOTS), BF),
            pltpu.VMEM((2, HD, SLOTS), F32),
            pltpu.VMEM((2, NY, CHUNK, HD), BF),
            pltpu.VMEM((2, NY, CHUNK, HD), F32),
            pltpu.VMEM((SHARD, HD), F32),
            pltpu.VMEM((2, NC, NY, CHUNK, HD), BF),
            pltpu.VMEM((2, NY, CHUNK, width), BF),
            pltpu.VMEM((2, NX, CHUNK, width), BF),
            pltpu.VMEM((CHUNK, width), BF),
            pltpu.VMEM((CHUNK, width), BF),
            pltpu.SemaphoreType.DMA((2, NY)),
            pltpu.SemaphoreType.DMA((2, NX)),
            pltpu.SemaphoreType.DMA((2,)),
        ]
        + (scatter_scratch() + gather_scratch()) * 2,
        compiler_params=pltpu.CompilerParams(collective_id=0, has_side_effects=True, vmem_limit_bytes=VMEM_LIMIT),
        name="cross",
    )(
        tile_turn, tile_len, query, grad_out, vision.reshape(NC, NY, CHUNK, width), w_key, w_value, text_turn, q_gain, k_gain
    )


def emit_kernel(*refs):
    count = len(refs) // 3
    sources, outs, held, sems = refs[:count], refs[count : 2 * count], refs[2 * count : 3 * count], refs[-1]
    pieces = []
    for i in range(count):
        rows = sources[i].shape[0]
        for start in range(0, rows, CHUNK):
            part = pl.ds(start, CHUNK)
            n = len(pieces)
            pieces.append(
                (
                    pltpu.make_async_copy(sources[i].at[part], held[i].at[part], sems.at[0, n]),
                    pltpu.make_async_copy(held[i].at[part], outs[i].at[part], sems.at[1, n]),
                )
            )
    for into, _ in pieces:
        into.start()
    for into, out in pieces:
        into.wait()
        out.start()
    for _, out in pieces:
        out.wait()


def emit(arrays):
    hbm = pl.BlockSpec(memory_space=pl.ANY)
    pieces = sum(a.shape[0] // CHUNK for a in arrays)
    return pl.pallas_call(
        emit_kernel,
        out_shape=tuple(jax.ShapeDtypeStruct(a.shape, a.dtype) for a in arrays),
        in_specs=[hbm] * len(arrays),
        out_specs=(hbm,) * len(arrays),
        scratch_shapes=[pltpu.VMEM(a.shape, a.dtype) for a in arrays] + [pltpu.SemaphoreType.DMA((2, pieces))],
        name="emit",
    )(*arrays)


def body(query, vision, w_key, w_value, q_gain, k_gain, text_turn, tile_turn, tile_len, grad_out):
    outs = cross(
        tile_turn, tile_len, query, grad_out, vision, w_key, w_value,
        text_turn.reshape(-1, HD), q_gain.reshape(1, HD), k_gain.reshape(1, HD),
    )
    return emit(outs)


def solution(mesh):
    return jax.shard_map(
        body,
        mesh=mesh,
        in_specs=(
            P("turn", "head"),
            P(None, "turn"),
            P("turn", "head"),
            P("turn", "head"),
            P(),
            P(),
            P("turn"),
            P(),
            P(),
            P("turn", "head"),
        ),
        out_specs=(
            P("turn", "head"),
            P("turn", "head"),
            P("head", "turn"),
            P("turn", "head"),
            P("turn", "head"),
        ),
        check_vma=False,
    )
```

```python
import math

import jax
import jax.numpy as jnp
from jax import lax
from jax.experimental import pallas as pl
from jax.experimental.pallas import tpu as pltpu
from jax.sharding import PartitionSpec as P

HD = 128
TILE_TOK = 256
TURNS = 64
EPS = 1e-05

NY, NZ, NC = 4, 8, 2
NHI, NX = 2, 4
CHUNK = 128
OWN_LO, OWNERS = 3, 2
SHARD = CHUNK // OWNERS
SLOTS = NC * NY * CHUNK

BF = jnp.bfloat16
F32 = jnp.float32
MESH = pl.DeviceIdType.MESH
SCALE = 1.0 / math.sqrt(HD)
LOG2E = math.log2(math.e)
MASKED = -16384.0
VMEM_LIMIT = 56 * 1024 * 1024

Y_ORDER = (2, 1, 3)
Y_ARRIVAL = (1, 3, 2)


def place():
    turn = lax.axis_index("turn")
    core = lax.rem(turn, NC)
    z = lax.rem(turn // NC, NZ)
    y = turn // (NC * NZ)
    return y, z, core


def turn_of(y, z, core):
    return (y * NZ + z) * NC + core


def is_owner(z):
    return jnp.logical_and(z >= OWN_LO, z < OWN_LO + OWNERS)


def remote(src, dst, send, recv, **where):
    return pltpu.make_async_remote_copy(
        src_ref=src, dst_ref=dst, send_sem=send, recv_sem=recv, device_id=where, device_id_type=MESH
    )


def scatter_scratch():
    return [
        pltpu.VMEM((2, NY, CHUNK, HD), BF),
        pltpu.VMEM((2, NY, CHUNK, HD), BF),
        pltpu.VMEM((2, NY - 1, CHUNK, HD), BF),
        pltpu.VMEM((2, OWNERS, SHARD, HD), F32),
        pltpu.VMEM((2, OWNERS, SHARD, HD), BF),
        pltpu.VMEM((2, NZ - 1, SHARD, HD), BF),
        pltpu.SemaphoreType.DMA((2, NY)),
        pltpu.SemaphoreType.DMA((2,)),
        pltpu.SemaphoreType.DMA((2,)),
        pltpu.SemaphoreType.DMA((3,)),
    ]


def gather_scratch():
    return [
        pltpu.VMEM((2, NC, NY, OWNERS, SHARD, HD), BF),
        pltpu.SemaphoreType.DMA((2,)),
        pltpu.SemaphoreType.DMA((2, NY)),
        pltpu.SemaphoreType.DMA((2, NY)),
        pltpu.SemaphoreType.DMA((3,)),
    ]


def foreign_scratch():
    return [
        pltpu.VMEM((2, NY, OWNERS, SHARD, HD), BF),
        pltpu.SemaphoreType.DMA((2,)),
        pltpu.SemaphoreType.DMA((2, NY)),
        pltpu.SemaphoreType.DMA((2, NY)),
        pltpu.SemaphoreType.DMA((3,)),
    ]


class Scatter:
    def __init__(self, refs, source, own):
        (self.from_c, self.to_y, self.from_y, self.total, self.to_z, self.from_z, self.rc, self.ry, self.rz, self.sent) = refs
        self.source = source
        self.own = own

    def core_copy(self, kind, off):
        y, z, core = place()
        yy = lax.rem(y + off, NY)
        return remote(
            self.source(kind, yy), self.from_c.at[kind, yy], self.sent.at[0], self.rc.at[kind, off],
            turn=turn_of(y, z, 1 - core),
        )

    def over_core(self, kind):
        y, z, core = place()
        for off in Y_ORDER + (0,):
            yy = lax.rem(y + off, NY)
            self.core_copy(kind, off).wait_recv()
            both = self.own(kind, yy).astype(F32) + self.from_c[kind, yy].astype(F32)
            if off == 0:
                self.total[kind] = both.reshape(OWNERS, SHARD, HD)
            else:
                self.to_y[kind, off] = both.astype(BF)
                remote(
                    self.to_y.at[kind, off], self.from_y.at[kind, off - 1], self.sent.at[1], self.ry.at[kind],
                    turn=turn_of(yy, z, core),
                ).start()

    def wait(self, ref, sem):
        y, z, core = place()
        remote(ref, ref, sem, sem, turn=turn_of(y, z, 1 - core)).wait_recv()

    def wait_sent(self, ref, sem):
        y, z, core = place()
        remote(ref, ref, sem, sem, turn=turn_of(y, z, 1 - core)).wait_send()

    def over_y(self, kind):
        y, z, core = place()
        self.wait(self.from_y.at[kind], self.ry.at[kind])
        total = self.total[kind].reshape(CHUNK, HD)
        for off in range(1, NY):
            total = total + self.from_y[kind, off - 1].astype(F32)
        total = total.reshape(OWNERS, SHARD, HD)
        self.total[kind] = total
        self.to_z[kind] = total.astype(BF)
        far = z // (NZ // 2)
        for step in range(OWNERS):
            owner = (OWNERS - 1 - step) * (1 - far) + step * far

            @pl.when(owner + OWN_LO != z)
            def _(owner=owner):
                slot = lax.rem(z - owner - OWN_LO + NZ + NZ - 1, NZ)
                remote(
                    self.to_z.at[kind, owner], self.from_z.at[kind, slot], self.sent.at[2], self.rz.at[kind],
                    turn=turn_of(y, owner + OWN_LO, core),
                ).start()

    def over_z(self, kind, then):
        y, z, core = place()

        @pl.when(is_owner(z))
        def _():
            total = self.total[kind, z - OWN_LO]
            self.wait(self.from_z.at[kind], self.rz.at[kind])
            for slot in range(NZ - 1):
                total = total + self.from_z[kind, slot].astype(F32)
            then(total)

    def finish(self):
        y, z, core = place()
        self.wait_sent(self.from_c, self.sent.at[0])
        self.wait_sent(self.from_y, self.sent.at[1])

        @pl.when(is_owner(z))
        def _():
            self.wait_sent(self.to_z.at[:, pl.ds(0, OWNERS - 1)], self.sent.at[2])

        @pl.when(jnp.logical_not(is_owner(z)))
        def _():
            self.wait_sent(self.to_z, self.sent.at[2])


class Gather:
    def __init__(self, refs):
        self.full, self.rz, self.ry, self.rc, self.sent = refs

    def chunk(self, kind, cc, yy):
        return self.full.at[kind, cc, yy]

    def over_z(self, kind, shard):
        y, z, core = place()
        self.full[kind, core, y, z - OWN_LO] = shard.astype(BF)
        src = self.full.at[kind, core, y, z - OWN_LO]
        for off in (4, 3, 5, 2, 6, 1, 7):
            remote(src, src, self.sent.at[0], self.rz.at[kind], turn=turn_of(y, lax.rem(z + off, NZ), core)).start()

    def wait(self, ref, sem):
        y, z, core = place()
        remote(ref, ref, sem, sem, turn=turn_of(y, z, 1 - core)).wait_recv()

    def wait_sent(self, ref, sem):
        y, z, core = place()
        remote(ref, ref, sem, sem, turn=turn_of(y, z, 1 - core)).wait_send()

    def over_y(self, kind):
        y, z, core = place()

        @pl.when(is_owner(z))
        def _():
            self.wait(self.full.at[kind, core, y, OWN_LO + OWNERS - 1 - z], self.rz.at[kind])

        @pl.when(jnp.logical_not(is_owner(z)))
        def _():
            self.wait(self.chunk(kind, core, y), self.rz.at[kind])

        self.spread(kind)

    def spread(self, kind):
        y, z, core = place()
        src = self.chunk(kind, core, y)
        for off in Y_ORDER:
            remote(src, src, self.sent.at[1], self.ry.at[kind, off], turn=turn_of(lax.rem(y + off, NY), z, core)).start()
        remote(src, src, self.sent.at[2], self.rc.at[kind, 0], turn=turn_of(y, z, 1 - core)).start()

    def over_core(self, kind, off):
        y, z, core = place()
        chunk = self.chunk(kind, core, lax.rem(y + NY - off, NY))
        self.wait(chunk, self.ry.at[kind, off])
        remote(chunk, chunk, self.sent.at[2], self.rc.at[kind, off], turn=turn_of(y, z, 1 - core)).start()

    def last(self, kind, off):
        y, z, core = place()
        self.wait(self.chunk(kind, 1 - core, lax.rem(y + NY - off, NY)), self.rc.at[kind, off])

    def finish(self, shards, chunks):
        y, z, core = place()

        @pl.when(is_owner(z))
        def _():
            self.wait_sent(shards, self.sent.at[0])

        self.wait_sent(chunks, self.sent.at[1])
        self.wait_sent(self.full.at[:, 0], self.sent.at[2])


class Foreign(Gather):
    def chunk(self, kind, cc, yy):
        return self.full.at[kind, yy]

    def over_z(self, kind, src, head):
        y, z, core = place()
        for zz in range(NZ):
            remote(
                src, self.full.at[kind, y, z - OWN_LO], self.sent.at[0], self.rz.at[kind],
                turn=turn_of(y, zz, core), head=head,
            ).start()

    def over_y(self, kind):
        y, z, core = place()
        self.wait(self.full.at[kind, y], self.rz.at[kind])
        self.spread(kind)


def inverse_rms(values):
    return lax.rsqrt(jnp.mean(values * values, axis=-1, keepdims=True) + EPS)


def rows_dot(a, b):
    return lax.dot_general(a, b, (((1,), (1,)), ((), ())), preferred_element_type=F32)


def columns_dot(a, b):
    return lax.dot_general(a, b, (((0,), (0,)), ((), ())), preferred_element_type=F32)


def cross_kernel(
    tile_turn, tile_len, query, grad_out, vision, w_key, w_value, text_turn, q_gain, k_gain,
    attended, grad_query, grad_vision, grad_w_key, grad_w_value,
    q_buf, up_buf, att_buf, gq_buf, s_io, qa, da, ka, va, inv, expo, slot_grad,
    weights_kv, to_c, own, raw, d_kv, to_x, from_x, far_weights, sx, sw, edge, ready, *scratch
):
    y, z, core = place()
    head = lax.axis_index("head")
    hi, x = head // NX, lax.rem(head, NX)
    rows, heads = q_buf.shape[0], q_buf.shape[1] // HD
    far_head = (1 - hi) * NX + x
    low, high = z == 0, z == NZ - 1
    at_edge = jnp.logical_or(low, high)
    my_edge = (z // (NZ // 2)) * (NZ - 1)

    barrier = pltpu.get_barrier_semaphore()

    def greet(**peer):
        pl.semaphore_signal(barrier, inc=1, device_id=peer, device_id_type=MESH)

    x_peers = [hi * NX + lax.rem(x + off, NX) for off in range(1, NX)]

    @pl.when(at_edge)
    def _():
        greet(turn=turn_of(y, NZ - 1 - z, core), head=far_head)

    @pl.when(jnp.logical_not(at_edge))
    def _():
        greet(turn=turn_of(y, my_edge, core))

    @pl.when(is_owner(z))
    def _():
        for off in range(1, NZ):
            greet(turn=turn_of(y, lax.rem(z + off, NZ), core))

    @pl.when(jnp.logical_not(is_owner(z)))
    def _():
        for owner in range(OWNERS):
            greet(turn=turn_of(y, owner + OWN_LO, core))

    for off in range(1, NY):
        greet(turn=turn_of(lax.rem(y + off, NY), z, core))
    for peer in x_peers:
        greet(head=peer)
    greet(turn=turn_of(y, z, 1 - core))

    load_query = pltpu.make_async_copy(query, q_buf, s_io.at[0])
    load_up = pltpu.make_async_copy(grad_out, up_buf, s_io.at[1])
    save_attended = pltpu.make_async_copy(att_buf, attended, s_io.at[2])
    save_grad = pltpu.make_async_copy(gq_buf, grad_query, s_io.at[3])
    load_query.start()
    load_up.start()

    def columns(h):
        return slice(None), pl.ds(pl.multiple_of(h * HD, HD), HD)

    weights_kv[:, :HD] = w_key[...]
    weights_kv[:, HD:] = w_value[...]

    def project(cc, out):
        both = jnp.dot(vision[cc].reshape(NY * CHUNK, vision.shape[-1]), weights_kv[...], preferred_element_type=F32)
        for kind in range(2):
            out[kind] = both[:, kind * HD : (kind + 1) * HD].reshape(NY, CHUNK, HD).astype(out.dtype)

    project(1 - core, to_c)
    project(core, own)

    for tile in range(SLOTS // TILE_TOK):
        inside = lax.broadcasted_iota(jnp.int32, (TILE_TOK, HD), 0)
        turn = lax.broadcasted_iota(jnp.int32, (TILE_TOK, HD), 1)
        shown = jnp.where(inside < tile_len[tile], tile_turn[tile], TURNS)
        hidden = jnp.logical_and(shown > turn, turn < TURNS)
        ka[pl.ds(tile * TILE_TOK, TILE_TOK), HD:] = jnp.where(hidden, MASKED, 0.0).astype(BF)
    va[:, HD:] = jnp.ones((SLOTS, HD), BF)
    for part in range(rows // HD):
        turn = lax.broadcasted_iota(jnp.int32, (HD, HD), 0)
        chosen = jnp.where(turn == text_turn[pl.ds(part, 1), :], 1.0, 0.0).T.astype(BF)
        for h in range(heads):
            qa[h, pl.ds(part * HD, HD), HD:] = chosen

    gain_q = q_gain[...]

    def norm_queries(h, carry):
        q_float = q_buf[columns(h)].astype(F32)
        inverse = inverse_rms(q_float)
        inv[h] = inverse
        qa[h, :, :HD] = (q_float * inverse * (gain_q * (SCALE * LOG2E))).astype(BF)
        return carry

    common = 1 + (NY - 1) + (NX - 1)
    ends = NZ // 2 - 1 + 1
    owner = is_owner(z)
    for here, count in (
        (owner, NZ - 1),
        (at_edge, OWNERS + ends),
        (jnp.logical_not(jnp.logical_or(owner, at_edge)), OWNERS),
    ):

        @pl.when(here)
        def _(count=count):
            pl.semaphore_wait(barrier, common + count)

    @pl.when(at_edge)
    def _():
        pl.semaphore_signal(
            edge, inc=1, device_id={"turn": turn_of(y, NZ - 1 - z, core), "head": far_head}, device_id_type=MESH
        )

    scatter = Scatter(scratch[:10], lambda kind, yy: to_c.at[kind, yy], lambda kind, yy: own[kind, yy])
    gather = Gather(scratch[10:15])
    for kind in range(2):
        for off in Y_ORDER + (0,):
            scatter.core_copy(kind, off).start()
    for kind in range(2):
        scatter.over_core(kind)
    load_query.wait()
    load_up.wait()
    lax.fori_loop(0, 3, norm_queries, 0)
    for kind in range(2):
        scatter.over_y(kind)
    lax.fori_loop(3, 6, norm_queries, 0)

    def key_shard(total):
        raw[...] = total
        gather.over_z(0, total * inverse_rms(total) * k_gain[...])

    scatter.over_z(0, key_shard)
    scatter.over_z(1, lambda total: gather.over_z(1, total))
    lax.fori_loop(6, heads, norm_queries, 0)
    for kind in range(2):
        gather.over_y(kind)
    for off in Y_ARRIVAL:
        for kind in range(2):
            gather.over_core(kind, off)
    for off in range(NY):
        for kind in range(2):
            gather.last(kind, off)

    @pl.when(at_edge)
    def _():
        pl.semaphore_wait(edge, 1)
        pl.semaphore_signal(ready, inc=1)
        for off in range(1, NZ):
            pl.semaphore_signal(
                ready, inc=1, device_id={"turn": turn_of(y, lax.rem(z + off, NZ), core)}, device_id_type=MESH
            )

    ka[:, :HD] = gather.full[0].reshape(SLOTS, HD)
    va[:, :HD] = gather.full[1].reshape(SLOTS, HD)

    lane = lax.broadcasted_iota(jnp.int32, (rows, HD), 1)
    slot_grad[...] = jnp.zeros_like(slot_grad)

    def forward(h):
        weights = jnp.exp2(rows_dot(qa[h], ka[...])).astype(BF)
        expo[h] = weights
        summed = jnp.dot(weights, va[...], preferred_element_type=F32)
        over = 1.0 / summed[:, HD:]
        att = (summed[:, :HD] * over).astype(BF)
        att_buf[columns(h)] = att
        up = up_buf[columns(h)].astype(F32)
        delta = -jnp.sum(up * att.astype(F32), axis=1, keepdims=True) * over
        high = delta.astype(BF)
        low = (delta - high.astype(F32)).astype(BF)
        up = (up * over).astype(BF)
        da[h, :, :HD] = up
        da[h, :, HD:] = jnp.where(lane == 0, high, jnp.where(lane == 1, low, jnp.zeros_like(low)))
        slot_grad[1] += columns_dot(up, weights)

    def forward_pair(pair, carry):
        for one in range(4):
            forward(4 * pair + one)
        return carry

    lax.fori_loop(0, heads // 4, forward_pair, 0)

    save_attended.start()
    sums = Scatter(
        scratch[15:25], lambda kind, yy: d_kv.at[kind, 1 - core, yy], lambda kind, yy: d_kv[kind, core, yy]
    )
    back = Gather(scratch[25:30])
    far = Foreign(scratch[30:35])

    def put(kind, factor):
        for cc in (1 - core, core):
            for off in Y_ORDER + (0,):
                yy = lax.rem(y + off, NY)
                start = pl.multiple_of((cc * NY + yy) * CHUNK, CHUNK)
                d_kv[kind, cc, yy] = (slot_grad[kind, :, pl.ds(start, CHUNK)] * factor).T.astype(BF)
                if cc is not core:
                    sums.core_copy(kind, off).start()

    put(1, 1.0)
    pl.semaphore_wait(ready, 2)
    for kind, weight in enumerate((w_key, w_value)):
        remote(weight, far_weights.at[kind], sw.at[0], sw.at[1], head=far_head).start()

    def backward(h):
        d_scores = expo[h] * rows_dot(da[h], va[...]).astype(BF)
        expo[h] = d_scores
        slot_grad[0] += columns_dot(qa[h, :, :HD], d_scores)

    def backward_pair(pair, carry):
        for one in range(4):
            backward(4 * pair + one)

        @pl.when(pair == 0)
        def _():
            sums.over_core(1)

        @pl.when(pair == 1)
        def _():
            sums.over_y(1)

        return carry

    lax.fori_loop(0, heads // 4, backward_pair, 0)
    put(0, 1.0 / LOG2E)

    def query_grad(h):
        d_query = jnp.dot(expo[h], ka[:, :HD], preferred_element_type=F32)
        q_float = q_buf[columns(h)].astype(F32)
        inverse = inv[h]
        scaled = d_query * (gain_q * SCALE)
        gq_buf[columns(h)] = (
            inverse * scaled - q_float * (inverse * inverse * inverse) * jnp.mean(q_float * scaled, axis=1, keepdims=True)
        ).astype(BF)

    def query_pair(pair, carry):
        query_grad(2 * pair)
        query_grad(2 * pair + 1)

        @pl.when(pair == 0)
        def _():
            sums.over_core(0)

        @pl.when(pair == 3)
        def _():
            sums.over_y(0)

        return carry

    lax.fori_loop(0, heads // 2, query_pair, 0)

    save_grad.start()

    def spread(kind, total):
        back.over_z(kind, total)

        @pl.when(core != hi)
        def _():
            far.over_z(kind, back.full.at[kind, core, y, z - OWN_LO], far_head)

    def key_grad_shard(total):
        raw_values = raw[...]
        inverse = inverse_rms(raw_values)
        scaled = total * k_gain[...]
        spread(
            0,
            inverse * scaled
            - raw_values * (inverse * inverse * inverse) * jnp.mean(raw_values * scaled, axis=1, keepdims=True),
        )

    sums.over_z(1, lambda total: spread(1, total))
    sums.over_z(0, key_grad_shard)
    direct, relayed = core == hi, core != hi

    def far_over_y(kind):
        @pl.when(direct)
        def _():
            far.over_y(kind)

    back.over_y(1)
    far_over_y(1)
    back.over_y(0)
    far_over_y(0)

    remote(far_weights, far_weights, sw.at[0], sw.at[1], head=far_head).wait_recv()

    def vision_term(off):
        yy = lax.rem(y + NY - off, NY)
        terms = [
            rows_dot(values.reshape(CHUNK, HD), weight)
            for values, weight in (
                (back.full[1, hi, yy], w_value[...]),
                (far.full[1, yy], far_weights[1]),
                (back.full[0, hi, yy], w_key[...]),
                (far.full[0, yy], far_weights[0]),
            )
        ]
        to_x[off] = (terms[0] + terms[1] + terms[2] + terms[3]).astype(BF)

        @pl.when(yy != x)
        def _():
            slot = lax.rem(yy - x + NX + NX - 1, NX)
            remote(to_x.at[off], from_x.at[slot], sx.at[0], sx.at[1], head=hi * NX + yy).start()

    for off in (0,) + Y_ARRIVAL:
        if off:
            for kind in (1, 0):
                back.over_core(kind, off)

        @pl.when(direct)
        def _(off=off):
            if off:
                for kind in (1, 0):
                    far.over_core(kind, off)
            vision_term(off)

    for off in (0,) + Y_ARRIVAL:
        for kind in (1, 0):
            back.last(kind, off)

        @pl.when(relayed)
        def _(off=off):
            for kind in (1, 0):
                far.last(kind, off)
            vision_term(off)

    for kind, out in ((0, grad_w_key), (1, grad_w_value)):
        out[...] = columns_dot(vision[...].reshape(SLOTS, vision.shape[-1]), back.full[kind].reshape(SLOTS, HD))
    total = to_x[lax.rem(y - x + NY, NY)].astype(F32)
    landed = from_x.at[pl.ds(0, NX - 1)]
    remote(landed, landed, sx.at[0], sx.at[1], head=x_peers[0]).wait_recv()
    for slot in range(NX - 1):
        total = total + from_x[slot].astype(F32)
    grad_vision[...] = total.astype(BF)

    remote(landed, landed, sx.at[0], sx.at[1], head=x_peers[0]).wait_send()
    remote(far_weights, far_weights, sw.at[0], sw.at[1], head=far_head).wait_send()
    scatter.finish()
    sums.finish()
    gather.finish(sums.from_z, sums.from_y)
    back.finish(sums.from_z, sums.from_y)

    @pl.when(direct)
    def _():
        far.wait_sent(sums.from_y, far.sent.at[1])
        far.wait_sent(far.full, far.sent.at[2])

    @pl.when(jnp.logical_and(relayed, is_owner(z)))
    def _():
        far.wait_sent(back.full.at[:, 0], far.sent.at[0])

    save_attended.wait()
    save_grad.wait()


def cross(tile_turn, tile_len, query, grad_out, vision, w_key, w_value, text_turn, q_gain, k_gain):
    vmem = pl.BlockSpec(memory_space=pltpu.VMEM)
    smem = pl.BlockSpec(memory_space=pltpu.SMEM)
    hbm = pl.BlockSpec(memory_space=pl.ANY)
    rows, columns = query.shape
    heads = columns // HD
    width = vision.shape[1]
    return pl.pallas_call(
        cross_kernel,
        out_shape=(
            jax.ShapeDtypeStruct(query.shape, BF),
            jax.ShapeDtypeStruct(query.shape, BF),
            jax.ShapeDtypeStruct((CHUNK, width), BF),
            jax.ShapeDtypeStruct((width, HD), F32),
            jax.ShapeDtypeStruct((width, HD), F32),
        ),
        in_specs=[smem, smem, hbm, hbm] + [vmem] * 6,
        out_specs=(hbm, hbm) + (vmem,) * 3,
        scratch_shapes=[
            pltpu.VMEM((rows, columns), BF),
            pltpu.VMEM((rows, columns), BF),
            pltpu.VMEM((rows, columns), BF),
            pltpu.VMEM((rows, columns), BF),
            pltpu.SemaphoreType.DMA((4,)),
            pltpu.VMEM((heads, rows, 2 * HD), BF),
            pltpu.VMEM((heads, rows, 2 * HD), BF),
            pltpu.VMEM((SLOTS, 2 * HD), BF),
            pltpu.VMEM((SLOTS, 2 * HD), BF),
            pltpu.VMEM((heads, rows, 1), F32),
            pltpu.VMEM((heads, rows, SLOTS), BF),
            pltpu.VMEM((2, HD, SLOTS), F32),
            pltpu.VMEM((HD, 2 * HD), BF),
            pltpu.VMEM((2, NY, CHUNK, HD), BF),
            pltpu.VMEM((2, NY, CHUNK, HD), F32),
            pltpu.VMEM((SHARD, HD), F32),
            pltpu.VMEM((2, NC, NY, CHUNK, HD), BF),
            pltpu.VMEM((NY, CHUNK, width), BF),
            pltpu.VMEM((NX, CHUNK, width), BF),
            pltpu.VMEM((2, width, HD), BF),
            pltpu.SemaphoreType.DMA((2,)),
            pltpu.SemaphoreType.DMA((2,)),
            pltpu.SemaphoreType.REGULAR,
            pltpu.SemaphoreType.REGULAR,
        ]
        + (scatter_scratch() + gather_scratch()) * 2
        + foreign_scratch(),
        compiler_params=pltpu.CompilerParams(collective_id=0, has_side_effects=True, vmem_limit_bytes=VMEM_LIMIT),
        name="cross",
    )(
        tile_turn, tile_len, query, grad_out, vision.reshape(NC, NY, CHUNK, width), w_key, w_value, text_turn, q_gain, k_gain
    )


def emit_kernel(*refs):
    count = len(refs) // 3
    sources, outs, held, sems = refs[:count], refs[count : 2 * count], refs[2 * count : 3 * count], refs[-1]
    pieces = []
    for i in range(count):
        rows = sources[i].shape[0]
        for start in range(0, rows, CHUNK):
            part = pl.ds(start, CHUNK)
            n = len(pieces)
            pieces.append(
                (
                    pltpu.make_async_copy(sources[i].at[part], held[i].at[part], sems.at[0, n]),
                    pltpu.make_async_copy(held[i].at[part], outs[i].at[part], sems.at[1, n]),
                )
            )
    for into, _ in pieces:
        into.start()
    for into, out in pieces:
        into.wait()
        out.start()
    for _, out in pieces:
        out.wait()


def emit(arrays):
    hbm = pl.BlockSpec(memory_space=pl.ANY)
    pieces = sum(a.shape[0] // CHUNK for a in arrays)
    return pl.pallas_call(
        emit_kernel,
        out_shape=tuple(jax.ShapeDtypeStruct(a.shape, a.dtype) for a in arrays),
        in_specs=[hbm] * len(arrays),
        out_specs=(hbm,) * len(arrays),
        scratch_shapes=[pltpu.VMEM(a.shape, a.dtype) for a in arrays] + [pltpu.SemaphoreType.DMA((2, pieces))],
        name="emit",
    )(*arrays)


def body(query, vision, w_key, w_value, q_gain, k_gain, text_turn, tile_turn, tile_len, grad_out):
    outs = cross(
        tile_turn, tile_len, query, grad_out, vision, w_key, w_value,
        text_turn.reshape(-1, HD), q_gain.reshape(1, HD), k_gain.reshape(1, HD),
    )
    return emit(outs)


def solution(mesh):
    return jax.shard_map(
        body,
        mesh=mesh,
        in_specs=(
            P("turn", "head"),
            P(None, "turn"),
            P("turn", "head"),
            P("turn", "head"),
            P(),
            P(),
            P("turn"),
            P(),
            P(),
            P("turn", "head"),
        ),
        out_specs=(
            P("turn", "head"),
            P("turn", "head"),
            P("head", "turn"),
            P("turn", "head"),
            P("turn", "head"),
        ),
        check_vma=False,
    )
```

```python
import math

import jax
import jax.numpy as jnp
from jax import lax
from jax.experimental import pallas as pl
from jax.experimental.pallas import tpu as pltpu
from jax.sharding import PartitionSpec as P

HD = 128
TILE_TOK = 256
TURNS = 64
EPS = 1e-05

NY, NZ, NC = 4, 8, 2
NHI, NX = 2, 4
CHUNK = 128
OWN_LO, OWNERS = 3, 2
SHARD = CHUNK // OWNERS
SLOTS = NC * NY * CHUNK

BF = jnp.bfloat16
F32 = jnp.float32
MESH = pl.DeviceIdType.MESH
SCALE = 1.0 / math.sqrt(HD)
LOG2E = math.log2(math.e)
MASKED = -16384.0
VMEM_LIMIT = 40 * 1024 * 1024

Y_ORDER = (2, 1, 3)
Y_ARRIVAL = (1, 3, 2)


def place():
    turn = lax.axis_index("turn")
    core = lax.rem(turn, NC)
    z = lax.rem(turn // NC, NZ)
    y = turn // (NC * NZ)
    return y, z, core


def turn_of(y, z, core):
    return (y * NZ + z) * NC + core


def is_owner(z):
    return jnp.logical_and(z >= OWN_LO, z < OWN_LO + OWNERS)


def remote(src, dst, send, recv, **where):
    return pltpu.make_async_remote_copy(
        src_ref=src, dst_ref=dst, send_sem=send, recv_sem=recv, device_id=where, device_id_type=MESH
    )


def scatter_scratch():
    return [
        pltpu.VMEM((2, NY, CHUNK, HD), BF),
        pltpu.VMEM((2, NY, CHUNK, HD), BF),
        pltpu.VMEM((2, NY - 1, CHUNK, HD), BF),
        pltpu.VMEM((2, OWNERS, SHARD, HD), F32),
        pltpu.VMEM((2, OWNERS, SHARD, HD), BF),
        pltpu.VMEM((2, NZ - 1, SHARD, HD), BF),
        pltpu.SemaphoreType.DMA((2, NY)),
        pltpu.SemaphoreType.DMA((2,)),
        pltpu.SemaphoreType.DMA((2,)),
        pltpu.SemaphoreType.DMA((3,)),
    ]


def gather_scratch():
    return [
        pltpu.VMEM((2, NC, NY, OWNERS, SHARD, HD), BF),
        pltpu.SemaphoreType.DMA((2,)),
        pltpu.SemaphoreType.DMA((2, NY)),
        pltpu.SemaphoreType.DMA((2, NY)),
        pltpu.SemaphoreType.DMA((3,)),
    ]


def foreign_scratch():
    return [
        pltpu.VMEM((2, NY, OWNERS, SHARD, HD), BF),
        pltpu.SemaphoreType.DMA((2,)),
        pltpu.SemaphoreType.DMA((2, NY)),
        pltpu.SemaphoreType.DMA((2,)),
    ]


class Scatter:
    def __init__(self, refs, source, own):
        (self.from_c, self.to_y, self.from_y, self.total, self.to_z, self.from_z, self.rc, self.ry, self.rz, self.sent) = refs
        self.source = source
        self.own = own

    def core_copy(self, kind, off):
        y, z, core = place()
        yy = lax.rem(y + off, NY)
        return remote(
            self.source(kind, yy), self.from_c.at[kind, yy], self.sent.at[0], self.rc.at[kind, off],
            turn=turn_of(y, z, 1 - core),
        )

    def over_core(self, kind):
        y, z, core = place()
        for off in Y_ORDER + (0,):
            yy = lax.rem(y + off, NY)
            self.core_copy(kind, off).wait_recv()
            both = self.own(kind, yy).astype(F32) + self.from_c[kind, yy].astype(F32)
            if off == 0:
                self.total[kind] = both.reshape(OWNERS, SHARD, HD)
            else:
                self.to_y[kind, off] = both.astype(BF)
                remote(
                    self.to_y.at[kind, off], self.from_y.at[kind, off - 1], self.sent.at[1], self.ry.at[kind],
                    turn=turn_of(yy, z, core),
                ).start()

    def wait(self, ref, sem):
        y, z, core = place()
        remote(ref, ref, sem, sem, turn=turn_of(y, z, 1 - core)).wait_recv()

    def wait_sent(self, ref, sem):
        y, z, core = place()
        remote(ref, ref, sem, sem, turn=turn_of(y, z, 1 - core)).wait_send()

    def over_y(self, kind):
        y, z, core = place()
        self.wait(self.from_y.at[kind], self.ry.at[kind])
        total = self.total[kind].reshape(CHUNK, HD)
        for off in range(1, NY):
            total = total + self.from_y[kind, off - 1].astype(F32)
        total = total.reshape(OWNERS, SHARD, HD)
        self.total[kind] = total
        self.to_z[kind] = total.astype(BF)
        far = z // (NZ // 2)
        for step in range(OWNERS):
            owner = (OWNERS - 1 - step) * (1 - far) + step * far

            @pl.when(owner + OWN_LO != z)
            def _(owner=owner):
                slot = lax.rem(z - owner - OWN_LO + NZ + NZ - 1, NZ)
                remote(
                    self.to_z.at[kind, owner], self.from_z.at[kind, slot], self.sent.at[2], self.rz.at[kind],
                    turn=turn_of(y, owner + OWN_LO, core),
                ).start()

    def over_z(self, kind, then):
        y, z, core = place()

        @pl.when(is_owner(z))
        def _():
            total = self.total[kind, z - OWN_LO]
            self.wait(self.from_z.at[kind], self.rz.at[kind])
            for slot in range(NZ - 1):
                total = total + self.from_z[kind, slot].astype(F32)
            then(total)

    def finish(self):
        y, z, core = place()
        self.wait_sent(self.from_c, self.sent.at[0])
        self.wait_sent(self.from_y, self.sent.at[1])

        @pl.when(is_owner(z))
        def _():
            self.wait_sent(self.to_z.at[:, pl.ds(0, OWNERS - 1)], self.sent.at[2])

        @pl.when(jnp.logical_not(is_owner(z)))
        def _():
            self.wait_sent(self.to_z, self.sent.at[2])


class Gather:
    def __init__(self, refs):
        self.full, self.rz, self.ry, self.rc, self.sent = refs

    def chunk(self, kind, cc, yy):
        return self.full.at[kind, cc, yy]

    def over_z(self, kind, shard):
        y, z, core = place()
        self.full[kind, core, y, z - OWN_LO] = shard.astype(BF)
        src = self.full.at[kind, core, y, z - OWN_LO]
        for off in (4, 3, 5, 2, 6, 1, 7):
            remote(src, src, self.sent.at[0], self.rz.at[kind], turn=turn_of(y, lax.rem(z + off, NZ), core)).start()

    def wait(self, ref, sem):
        y, z, core = place()
        remote(ref, ref, sem, sem, turn=turn_of(y, z, 1 - core)).wait_recv()

    def wait_sent(self, ref, sem):
        y, z, core = place()
        remote(ref, ref, sem, sem, turn=turn_of(y, z, 1 - core)).wait_send()

    def over_y(self, kind):
        y, z, core = place()

        @pl.when(is_owner(z))
        def _():
            self.wait(self.full.at[kind, core, y, OWN_LO + OWNERS - 1 - z], self.rz.at[kind])

        @pl.when(jnp.logical_not(is_owner(z)))
        def _():
            self.wait(self.chunk(kind, core, y), self.rz.at[kind])

        self.spread(kind)

    def spread_y(self, kind):
        y, z, core = place()
        src = self.chunk(kind, core, y)
        for off in Y_ORDER:
            remote(src, src, self.sent.at[1], self.ry.at[kind, off], turn=turn_of(lax.rem(y + off, NY), z, core)).start()

    def spread(self, kind):
        y, z, core = place()
        self.spread_y(kind)
        src = self.chunk(kind, core, y)
        remote(src, src, self.sent.at[2], self.rc.at[kind, 0], turn=turn_of(y, z, 1 - core)).start()

    def over_core(self, kind, off):
        y, z, core = place()
        chunk = self.chunk(kind, core, lax.rem(y + NY - off, NY))
        self.wait(chunk, self.ry.at[kind, off])
        remote(chunk, chunk, self.sent.at[2], self.rc.at[kind, off], turn=turn_of(y, z, 1 - core)).start()

    def last(self, kind, off):
        y, z, core = place()
        self.wait(self.chunk(kind, 1 - core, lax.rem(y + NY - off, NY)), self.rc.at[kind, off])

    def finish(self, shards, chunks):
        y, z, core = place()

        @pl.when(is_owner(z))
        def _():
            self.wait_sent(shards, self.sent.at[0])

        self.wait_sent(chunks, self.sent.at[1])
        self.wait_sent(self.full.at[:, 0], self.sent.at[2])


class Foreign(Gather):
    def __init__(self, refs):
        self.full, self.rz, self.ry, self.sent = refs

    def chunk(self, kind, cc, yy):
        return self.full.at[kind, yy]

    def over_z(self, kind, src, head):
        y, z, core = place()
        for zz in range(NZ):
            remote(
                src, self.full.at[kind, y, z - OWN_LO], self.sent.at[0], self.rz.at[kind],
                turn=turn_of(y, zz, core), head=head,
            ).start()

    def over_y(self, kind):
        y, z, core = place()
        self.wait(self.full.at[kind, y], self.rz.at[kind])
        self.spread_y(kind)

    def arrived(self, kind, off):
        y, z, core = place()
        self.wait(self.chunk(kind, core, lax.rem(y + NY - off, NY)), self.ry.at[kind, off])


def inverse_rms(values):
    return lax.rsqrt(jnp.mean(values * values, axis=-1, keepdims=True) + EPS)


def rows_dot(a, b):
    return lax.dot_general(a, b, (((1,), (1,)), ((), ())), preferred_element_type=F32)


def columns_dot(a, b):
    return lax.dot_general(a, b, (((0,), (0,)), ((), ())), preferred_element_type=F32)


def cross_kernel(
    tile_turn_in, tile_len_in, query, grad_out, vision_in, w_key_in, w_value_in, text_turn_in, q_gain_in, k_gain_in,
    att_buf, gq_buf, grad_vision, grad_w_key, grad_w_value,
    q_buf, up_buf, vision, w_key, w_value, text_turn, q_gain, k_gain, tile_turn, tile_len, s_io, qa, da, ka, va, inv, expo, slot_grad,
    weights_kv, vision_t, v_terms, to_c, own, raw, d_kv, to_x, from_x, near_weights, far_weights, sx, sn, sw, edge, beside, ready, *scratch
):
    y, z, core = place()
    head = lax.axis_index("head")
    hi, x = head // NX, lax.rem(head, NX)
    rows, heads = q_buf.shape[0], q_buf.shape[1] // HD
    far_head = (1 - hi) * NX + x
    low, high = z == 0, z == NZ - 1
    at_edge = jnp.logical_or(low, high)
    my_edge = (z // (NZ // 2)) * (NZ - 1)

    barrier = pltpu.get_barrier_semaphore()

    def greet(**peer):
        pl.semaphore_signal(barrier, inc=1, device_id=peer, device_id_type=MESH)

    x_peers = [hi * NX + lax.rem(x + off, NX) for off in range(1, NX)]

    @pl.when(at_edge)
    def _():
        greet(turn=turn_of(y, NZ - 1 - z, core), head=far_head)

    @pl.when(jnp.logical_not(at_edge))
    def _():
        greet(turn=turn_of(y, my_edge, core))

    @pl.when(is_owner(z))
    def _():
        for off in range(1, NZ):
            greet(turn=turn_of(y, lax.rem(z + off, NZ), core))

    @pl.when(jnp.logical_not(is_owner(z)))
    def _():
        for owner in range(OWNERS):
            greet(turn=turn_of(y, owner + OWN_LO, core))

    for off in range(1, NY):
        greet(turn=turn_of(lax.rem(y + off, NY), z, core))

    @pl.when(z == OWN_LO)
    def _():
        for peer in x_peers:
            greet(head=peer)

    greet(turn=turn_of(y, z, 1 - core))

    loads = [
        pltpu.make_async_copy(src, dst, s_io.at[n])
        for n, (src, dst) in enumerate(
            (
                (vision_in, vision), (w_key_in, w_key), (w_value_in, w_value), (tile_turn_in, tile_turn), (tile_len_in, tile_len),
                (text_turn_in, text_turn), (q_gain_in, q_gain), (k_gain_in, k_gain), (query, q_buf), (grad_out, up_buf),
            )
        )
    ]
    for load in loads:
        load.start()

    def columns(h):
        return slice(None), pl.ds(pl.multiple_of(h * HD, HD), HD)

    for load in loads[:3]:
        load.wait()
    weights_kv[:, :HD] = w_key[...]
    weights_kv[:, HD:] = w_value[...]

    def project(cc, out):
        both = jnp.dot(vision[cc].reshape(NY * CHUNK, vision.shape[-1]), weights_kv[...], preferred_element_type=F32)
        for kind in range(2):
            out[kind] = both[:, kind * HD : (kind + 1) * HD].reshape(NY, CHUNK, HD).astype(out.dtype)

    project(1 - core, to_c)
    project(core, own)

    def norm_queries(h, carry):
        gain_q = q_gain[...]
        q_float = q_buf[columns(h)].astype(F32)
        inverse = inverse_rms(q_float)
        inv[h] = inverse
        qa[h, :, :HD] = (q_float * inverse * (gain_q * (SCALE * LOG2E))).astype(BF)
        return carry

    common = 1 + (NY - 1)
    ends = NZ // 2 - 1 + 1
    owner = is_owner(z)
    for here, count in (
        (z == OWN_LO, NZ - 1 + NX - 1),
        (jnp.logical_and(owner, z != OWN_LO), NZ - 1),
        (at_edge, OWNERS + ends),
        (jnp.logical_not(jnp.logical_or(owner, at_edge)), OWNERS),
    ):

        @pl.when(here)
        def _(count=count):
            pl.semaphore_wait(barrier, common + count)

    @pl.when(at_edge)
    def _():
        pl.semaphore_signal(
            edge, inc=1, device_id={"turn": turn_of(y, NZ - 1 - z, core), "head": far_head}, device_id_type=MESH
        )

    @pl.when(z == OWN_LO)
    def _():
        for peer in x_peers:
            pl.semaphore_signal(beside, inc=1, device_id={"head": peer}, device_id_type=MESH)

    scatter = Scatter(scratch[:10], lambda kind, yy: to_c.at[kind, yy], lambda kind, yy: own[kind, yy])
    gather = Gather(scratch[10:15])
    for kind in range(2):
        for off in Y_ORDER + (0,):
            scatter.core_copy(kind, off).start()
    for kind, weight in enumerate((w_key, w_value)):
        near_weights[kind, 0] = weight[...]
        remote(weight, near_weights.at[kind, 1], sn.at[0], sn.at[1], turn=turn_of(y, z, 1 - core)).start()
    scatter.over_core(0)
    for load in loads[3:]:
        load.wait()
    for tile in range(SLOTS // TILE_TOK):
        inside = lax.broadcasted_iota(jnp.int32, (TILE_TOK, HD), 0)
        turn = lax.broadcasted_iota(jnp.int32, (TILE_TOK, HD), 1)
        shown = jnp.where(inside < tile_len[tile], tile_turn[tile], TURNS)
        hidden = jnp.logical_and(shown > turn, turn < TURNS)
        ka[pl.ds(tile * TILE_TOK, TILE_TOK), HD:] = jnp.where(hidden, MASKED, 0.0).astype(BF)
    va[:, HD:] = jnp.ones((SLOTS, HD), BF)
    vision_t[...] = vision[...].reshape(SLOTS, vision.shape[-1]).T
    for part in range(rows // HD):
        turn = lax.broadcasted_iota(jnp.int32, (HD, HD), 0)
        chosen = jnp.where(turn == text_turn[pl.ds(part, 1), :], 1.0, 0.0).T.astype(BF)
        for h in range(heads):
            qa[h, pl.ds(part * HD, HD), HD:] = chosen

    lax.fori_loop(0, 3, norm_queries, 0)
    scatter.over_y(0)
    scatter.over_core(1)
    lax.fori_loop(3, heads, norm_queries, 0)

    def key_shard(total):
        raw[...] = total
        gather.over_z(0, total * inverse_rms(total) * k_gain[...])

    scatter.over_z(0, key_shard)
    scatter.over_y(1)
    gather.over_y(0)
    scatter.over_z(1, lambda total: gather.over_z(1, total))
    for off in Y_ARRIVAL:
        gather.over_core(0, off)
    gather.over_y(1)
    for off in range(NY):
        gather.last(0, off)
    ka[:, :HD] = gather.full[0].reshape(SLOTS, HD)

    def score(h):
        expo[h] = jnp.exp2(rows_dot(qa[h], ka[...])).astype(BF)

    def score_pair(pair, carry):
        score(2 * pair)
        score(2 * pair + 1)

        @pl.when(pair == 1)
        def _():
            for off in Y_ARRIVAL:
                gather.over_core(1, off)

        return carry

    lax.fori_loop(0, heads // 2, score_pair, 0)
    for off in range(NY):
        gather.last(1, off)

    @pl.when(z == OWN_LO)
    def _():
        pl.semaphore_wait(beside, NX - 1)

    @pl.when(at_edge)
    def _():
        pl.semaphore_wait(edge, 1)

    @pl.when(jnp.logical_or(z == OWN_LO, at_edge))
    def _():
        pl.semaphore_signal(ready, inc=1)
        for off in range(1, NZ):
            pl.semaphore_signal(
                ready, inc=1, device_id={"turn": turn_of(y, lax.rem(z + off, NZ), core)}, device_id_type=MESH
            )

    va[:, :HD] = gather.full[1].reshape(SLOTS, HD)

    lane = lax.broadcasted_iota(jnp.int32, (rows, HD), 1)
    slot_grad[...] = jnp.zeros_like(slot_grad)

    def forward(h):
        weights = expo[h]
        summed = jnp.dot(weights, va[...], preferred_element_type=F32)
        over = 1.0 / summed[:, HD:]
        att = (summed[:, :HD] * over).astype(BF)
        att_buf[columns(h)] = att
        up = up_buf[columns(h)].astype(F32)
        delta = -jnp.sum(up * att.astype(F32), axis=1, keepdims=True) * over
        high = delta.astype(BF)
        low = (delta - high.astype(F32)).astype(BF)
        up = (up * over).astype(BF)
        da[h, :, :HD] = up
        da[h, :, HD:] = jnp.where(lane == 0, high, jnp.where(lane == 1, low, jnp.zeros_like(low)))
        slot_grad[1] += columns_dot(up, weights)

    def forward_pair(pair, carry):
        for one in range(4):
            forward(4 * pair + one)
        return carry

    lax.fori_loop(0, heads // 4, forward_pair, 0)

    sums = Scatter(
        scratch[15:25], lambda kind, yy: d_kv.at[kind, 1 - core, yy], lambda kind, yy: d_kv[kind, core, yy]
    )
    back = Gather(scratch[25:30])
    far = Foreign(scratch[30:35])

    def put(kind, factor):
        for cc in (1 - core, core):
            for off in Y_ORDER + (0,):
                yy = lax.rem(y + off, NY)
                start = pl.multiple_of((cc * NY + yy) * CHUNK, CHUNK)
                d_kv[kind, cc, yy] = (slot_grad[kind, :, pl.ds(start, CHUNK)] * factor).T.astype(BF)
                if cc is not core:
                    sums.core_copy(kind, off).start()

    put(1, 1.0)
    pl.semaphore_wait(ready, 3)
    from_core = near_weights.at[:, 1]
    remote(from_core, from_core, sn.at[0], sn.at[1], turn=turn_of(y, z, 1 - core)).wait()

    direct, relayed = core == hi, core != hi

    @pl.when(relayed)
    def _():
        for kind in range(2):
            remote(near_weights.at[kind], far_weights.at[kind], sw.at[0], sw.at[1], head=far_head).start()

    def backward(h):
        d_scores = expo[h] * rows_dot(da[h], va[...]).astype(BF)
        expo[h] = d_scores
        slot_grad[0] += columns_dot(qa[h, :, :HD], d_scores)

    def backward_pair(pair, carry):
        backward(2 * pair)
        backward(2 * pair + 1)

        @pl.when(pair == 0)
        def _():
            sums.over_core(1)

        @pl.when(pair == 3)
        def _():
            sums.over_y(1)

        return carry

    lax.fori_loop(0, heads // 2, backward_pair, 0)
    put(0, 1.0 / LOG2E)

    def spread(kind, total):
        back.over_z(kind, total)

        @pl.when(core != hi)
        def _():
            far.over_z(kind, back.full.at[kind, core, y, z - OWN_LO], far_head)

    def query_grad(h):
        d_query = jnp.dot(expo[h], ka[:, :HD], preferred_element_type=F32)
        q_float = q_buf[columns(h)].astype(F32)
        inverse = inv[h]
        scaled = d_query * (q_gain[...] * SCALE)
        gq_buf[columns(h)] = (
            inverse * scaled - q_float * (inverse * inverse * inverse) * jnp.mean(q_float * scaled, axis=1, keepdims=True)
        ).astype(BF)

    def query_pair(pair, carry):
        query_grad(2 * pair)
        query_grad(2 * pair + 1)

        @pl.when(pair == 0)
        def _():
            sums.over_core(0)

        @pl.when(pair == 2)
        def _():
            sums.over_z(1, lambda total: spread(1, total))

        @pl.when(pair == 3)
        def _():
            sums.over_y(0)

        return carry

    lax.fori_loop(0, heads // 2, query_pair, 0)


    def key_grad_shard(total):
        raw_values = raw[...]
        inverse = inverse_rms(raw_values)
        scaled = total * k_gain[...]
        spread(
            0,
            inverse * scaled
            - raw_values * (inverse * inverse * inverse) * jnp.mean(raw_values * scaled, axis=1, keepdims=True),
        )

    sums.over_z(0, key_grad_shard)
    def far_over_y(kind):
        @pl.when(direct)
        def _():
            far.over_y(kind)

    def vision_term(kind, off):
        yy = lax.rem(y + NY - off, NY)
        return rows_dot(
            back.full[kind, hi, yy].reshape(CHUNK, HD), near_weights[kind].reshape(NC * CHUNK, HD)
        ) + rows_dot(far.full[kind, yy].reshape(CHUNK, HD), far_weights[kind].reshape(NC * CHUNK, HD))

    def send_terms(off):
        yy = lax.rem(y + NY - off, NY)
        both = v_terms[off] + vision_term(0, off)
        slot = lax.rem(yy - x + NX + NX - 1, NX)
        width = vision.shape[-1]
        to_x[NC * off] = both[:, :width].astype(BF)
        to_x[NC * off + 1] = both[:, width:].astype(BF)
        remote(
            to_x.at[NC * off + 1], from_x.at[slot], sx.at[0], sx.at[1], turn=turn_of(y, z, 1 - core), head=hi * NX + yy
        ).start()

        @pl.when(yy != x)
        def _():
            remote(to_x.at[NC * off], from_x.at[slot], sx.at[0], sx.at[1], head=hi * NX + yy).start()

    def weight_grad(kind, out):
        out[...] = jnp.dot(vision_t[...], back.full[kind].reshape(SLOTS, HD), preferred_element_type=F32)

    back.over_y(1)
    far_over_y(1)
    back.over_y(0)
    for off in Y_ARRIVAL:
        back.over_core(1, off)

    @pl.when(direct)
    def _():
        remote(far_weights, far_weights, sw.at[0], sw.at[1], head=far_head).wait_recv()
        for off in Y_ARRIVAL:
            far.arrived(1, off)

    far_over_y(0)

    @pl.when(direct)
    def _():
        for off in range(NY):
            v_terms[off] = vision_term(1, off)

    for off in range(NY):
        back.last(1, off)
    weight_grad(1, grad_w_value)

    for off in (0,) + Y_ARRIVAL:
        if off:
            back.over_core(0, off)

        @pl.when(direct)
        def _(off=off):
            if off:
                far.arrived(0, off)
            send_terms(off)

    for off in range(NY):
        back.last(0, off)
    weight_grad(0, grad_w_key)

    scatter.finish()
    sums.finish()
    gather.finish(sums.from_z, sums.from_y)
    back.finish(sums.from_z, sums.from_y)

    @pl.when(direct)
    def _():
        far.wait_sent(sums.from_y, far.sent.at[1])

    @pl.when(relayed)
    def _():
        remote(near_weights, near_weights, sw.at[0], sw.at[1], head=far_head).wait_send()

    @pl.when(jnp.logical_and(relayed, is_owner(z)))
    def _():
        far.wait_sent(back.full.at[:, 0], far.sent.at[0])

    def landed(count):
        part = from_x.at[pl.ds(0, count)]
        remote(part, part, sx.at[0], sx.at[1], head=x_peers[0]).wait_recv()
        total = from_x[0].astype(F32)
        for slot in range(1, count):
            total = total + from_x[slot].astype(F32)
        return total

    @pl.when(direct)
    def _():
        sent = to_x.at[pl.ds(0, NC * NY - 1)]
        remote(sent, sent, sx.at[0], sx.at[1], head=x_peers[0]).wait_send()
        grad_vision[...] = (landed(NX - 1) + to_x[NC * lax.rem(y - x + NY, NY)].astype(F32)).astype(BF)

    @pl.when(relayed)
    def _():
        grad_vision[...] = landed(NX).astype(BF)


def cross(tile_turn, tile_len, query, grad_out, vision, w_key, w_value, text_turn, q_gain, k_gain):
    vmem = pl.BlockSpec(memory_space=pltpu.VMEM)
    hbm = pl.BlockSpec(memory_space=pltpu.HBM)
    rows, columns = query.shape
    heads = columns // HD
    width = vision.shape[1]
    return pl.pallas_call(
        cross_kernel,
        out_shape=(
            jax.ShapeDtypeStruct(query.shape, BF),
            jax.ShapeDtypeStruct(query.shape, BF),
            jax.ShapeDtypeStruct((CHUNK, width), BF),
            jax.ShapeDtypeStruct((width, HD), F32),
            jax.ShapeDtypeStruct((width, HD), F32),
        ),
        in_specs=[hbm] * 10,
        out_specs=(vmem,) * 5,
        scratch_shapes=[
            pltpu.VMEM((rows, columns), BF),
            pltpu.VMEM((rows, columns), BF),
            pltpu.VMEM((NC, NY, CHUNK, width), BF),
            pltpu.VMEM((width, HD), BF),
            pltpu.VMEM((width, HD), BF),
            pltpu.VMEM((rows // HD, HD), jnp.int32),
            pltpu.VMEM((1, HD), F32),
            pltpu.VMEM((1, HD), F32),
            pltpu.SMEM((SLOTS // TILE_TOK,), jnp.int32),
            pltpu.SMEM((SLOTS // TILE_TOK,), jnp.int32),
            pltpu.SemaphoreType.DMA((10,)),
            pltpu.VMEM((heads, rows, 2 * HD), BF),
            pltpu.VMEM((heads, rows, 2 * HD), BF),
            pltpu.VMEM((SLOTS, 2 * HD), BF),
            pltpu.VMEM((SLOTS, 2 * HD), BF),
            pltpu.VMEM((heads, rows, 1), F32),
            pltpu.VMEM((heads, rows, SLOTS), BF),
            pltpu.VMEM((2, HD, SLOTS), F32),
            pltpu.VMEM((HD, 2 * HD), BF),
            pltpu.VMEM((width, SLOTS), BF),
            pltpu.VMEM((NY, CHUNK, NC * width), F32),
            pltpu.VMEM((2, NY, CHUNK, HD), BF),
            pltpu.VMEM((2, NY, CHUNK, HD), F32),
            pltpu.VMEM((SHARD, HD), F32),
            pltpu.VMEM((2, NC, NY, CHUNK, HD), BF),
            pltpu.VMEM((NY * NC, CHUNK, width), BF),
            pltpu.VMEM((NX, CHUNK, width), BF),
            pltpu.VMEM((2, NC, width, HD), BF),
            pltpu.VMEM((2, NC, width, HD), BF),
            pltpu.SemaphoreType.DMA((2,)),
            pltpu.SemaphoreType.DMA((2,)),
            pltpu.SemaphoreType.DMA((2,)),
            pltpu.SemaphoreType.REGULAR,
            pltpu.SemaphoreType.REGULAR,
            pltpu.SemaphoreType.REGULAR,
        ]
        + (scatter_scratch() + gather_scratch()) * 2
        + foreign_scratch(),
        compiler_params=pltpu.CompilerParams(collective_id=0, has_side_effects=True, vmem_limit_bytes=VMEM_LIMIT),
        name="cross",
    )(
        *(
            pltpu.with_memory_space_constraint(operand, pltpu.HBM)
            for operand in (
                tile_turn, tile_len, query, grad_out, vision.reshape(NC, NY, CHUNK, width), w_key, w_value, text_turn,
                q_gain, k_gain,
            )
        )
    )


def emit_kernel(*refs):
    count = len(refs) // 2
    copies = []
    for i in range(count):
        for start in range(0, refs[i].shape[0], CHUNK):
            part = pl.ds(start, CHUNK)
            copies.append(pltpu.make_async_copy(refs[i].at[part], refs[count + i].at[part], refs[-1].at[len(copies)]))
    for copy in copies:
        copy.start()
    for copy in copies:
        copy.wait()


def emit(arrays):
    vmem = pl.BlockSpec(memory_space=pltpu.VMEM)
    hbm = pl.BlockSpec(memory_space=pltpu.HBM)
    return pl.pallas_call(
        emit_kernel,
        out_shape=tuple(jax.ShapeDtypeStruct(a.shape, a.dtype) for a in arrays),
        in_specs=[vmem] * len(arrays),
        out_specs=(hbm,) * len(arrays),
        scratch_shapes=[pltpu.SemaphoreType.DMA((sum(a.shape[0] // CHUNK for a in arrays),))],
        compiler_params=pltpu.CompilerParams(vmem_limit_bytes=8 * 1024 * 1024),
        name="emit",
    )(*arrays)


def body(query, vision, w_key, w_value, q_gain, k_gain, text_turn, tile_turn, tile_len, grad_out):
    outs = cross(
        tile_turn, tile_len, query, grad_out, vision, w_key, w_value,
        text_turn.reshape(-1, HD), q_gain.reshape(1, HD), k_gain.reshape(1, HD),
    )
    return emit(outs)


def solution(mesh):
    return jax.shard_map(
        body,
        mesh=mesh,
        in_specs=(
            P("turn", "head"),
            P(None, "turn"),
            P("turn", "head"),
            P("turn", "head"),
            P(),
            P(),
            P("turn"),
            P(),
            P(),
            P("turn", "head"),
        ),
        out_specs=(
            P("turn", "head"),
            P("turn", "head"),
            P("head", "turn"),
            P("turn", "head"),
            P("turn", "head"),
        ),
        check_vma=False,
    )
```

```python
import math

import jax
import jax.numpy as jnp
from jax import lax
from jax.experimental import pallas as pl
from jax.experimental.pallas import tpu as pltpu
from jax.sharding import PartitionSpec as P

HD = 128
TILE_TOK = 256
TURNS = 64
EPS = 1e-05

NY, NZ, NC = 4, 8, 2
NHI, NX = 2, 4
CHUNK = 128
OWN_LO, OWNERS = 3, 2
SHARD = CHUNK // OWNERS
SLOTS = NC * NY * CHUNK

BF = jnp.bfloat16
F32 = jnp.float32
MESH = pl.DeviceIdType.MESH
SCALE = 1.0 / math.sqrt(HD)
LOG2E = math.log2(math.e)
MASKED = -16384.0
VMEM_LIMIT = 40 * 1024 * 1024

Y_ORDER = (2, 1, 3)
Y_ARRIVAL = (1, 3, 2)


def place():
    turn = lax.axis_index("turn")
    core = lax.rem(turn, NC)
    z = lax.rem(turn // NC, NZ)
    y = turn // (NC * NZ)
    return y, z, core


def turn_of(y, z, core):
    return (y * NZ + z) * NC + core


def is_owner(z):
    return jnp.logical_and(z >= OWN_LO, z < OWN_LO + OWNERS)


def remote(src, dst, send, recv, **where):
    return pltpu.make_async_remote_copy(
        src_ref=src, dst_ref=dst, send_sem=send, recv_sem=recv, device_id=where, device_id_type=MESH
    )


def nearest(z, step):
    far = z // (NZ // 2)
    return step * (1 - far) + (OWNERS - 1 - step) * far


def scatter_scratch():
    return [
        pltpu.VMEM((2, NY, CHUNK, HD), BF),
        pltpu.VMEM((2, NY, OWNERS, SHARD, HD), BF),
        pltpu.VMEM((2, OWNERS, NY - 1, SHARD, HD), BF),
        pltpu.VMEM((2, OWNERS, SHARD, HD), F32),
        pltpu.VMEM((2, OWNERS, SHARD, HD), BF),
        pltpu.VMEM((2, NZ - 1, SHARD, HD), BF),
        pltpu.SemaphoreType.DMA((2, NY)),
        pltpu.SemaphoreType.DMA((2, OWNERS)),
        pltpu.SemaphoreType.DMA((2,)),
        pltpu.SemaphoreType.DMA((3,)),
    ]


def gather_scratch():
    return [
        pltpu.VMEM((2, NC, NY, OWNERS, SHARD, HD), BF),
        pltpu.SemaphoreType.DMA((2, OWNERS)),
        pltpu.SemaphoreType.DMA((2, NY)),
        pltpu.SemaphoreType.DMA((2, NY)),
        pltpu.SemaphoreType.DMA((3,)),
    ]


def foreign_scratch():
    return [
        pltpu.VMEM((2, NY, OWNERS, SHARD, HD), BF),
        pltpu.SemaphoreType.DMA((2, OWNERS)),
        pltpu.SemaphoreType.DMA((2, NY)),
        pltpu.SemaphoreType.DMA((2,)),
    ]


class Scatter:
    def __init__(self, refs, source, own):
        (self.from_c, self.to_y, self.from_y, self.total, self.to_z, self.from_z, self.rc, self.ry, self.rz, self.sent) = refs
        self.source = source
        self.own = own

    def core_copy(self, kind, off):
        y, z, core = place()
        yy = lax.rem(y + off, NY)
        return remote(
            self.source(kind, yy), self.from_c.at[kind, yy], self.sent.at[0], self.rc.at[kind, off],
            turn=turn_of(y, z, 1 - core),
        )

    def over_core(self, kind):
        y, z, core = place()
        for off in Y_ORDER + (0,):
            yy = lax.rem(y + off, NY)
            self.core_copy(kind, off).wait_recv()
            both = self.own(kind, yy).astype(F32) + self.from_c[kind, yy].astype(F32)
            both = both.reshape(OWNERS, SHARD, HD)
            if off == 0:
                self.total[kind] = both
            else:
                self.to_y[kind, off] = both.astype(BF)
        for step in reversed(range(OWNERS)):
            owner = nearest(z, step)
            for off in Y_ORDER:
                remote(
                    self.to_y.at[kind, off, owner], self.from_y.at[kind, owner, off - 1], self.sent.at[1],
                    self.ry.at[kind, owner], turn=turn_of(lax.rem(y + off, NY), z, core),
                ).start()

    def wait(self, ref, sem):
        y, z, core = place()
        remote(ref, ref, sem, sem, turn=turn_of(y, z, 1 - core)).wait_recv()

    def wait_sent(self, ref, sem):
        y, z, core = place()
        remote(ref, ref, sem, sem, turn=turn_of(y, z, 1 - core)).wait_send()

    def over_y(self, kind):
        y, z, core = place()
        for step in reversed(range(OWNERS)):
            owner = nearest(z, step)
            self.wait(self.from_y.at[kind, owner], self.ry.at[kind, owner])
            total = self.total[kind, owner]
            for off in range(1, NY):
                total = total + self.from_y[kind, owner, off - 1].astype(F32)
            self.total[kind, owner] = total
            self.to_z[kind, owner] = total.astype(BF)

            @pl.when(owner + OWN_LO != z)
            def _(owner=owner):
                slot = lax.rem(z - owner - OWN_LO + NZ + NZ - 1, NZ)
                remote(
                    self.to_z.at[kind, owner], self.from_z.at[kind, slot], self.sent.at[2], self.rz.at[kind],
                    turn=turn_of(y, owner + OWN_LO, core),
                ).start()

    def over_z(self, kind, then):
        y, z, core = place()

        @pl.when(is_owner(z))
        def _():
            total = self.total[kind, z - OWN_LO]
            self.wait(self.from_z.at[kind], self.rz.at[kind])
            for slot in range(NZ - 1):
                total = total + self.from_z[kind, slot].astype(F32)
            then(total)

    def finish(self):
        y, z, core = place()
        self.wait_sent(self.from_c, self.sent.at[0])
        self.wait_sent(self.from_y, self.sent.at[1])

        @pl.when(is_owner(z))
        def _():
            self.wait_sent(self.to_z.at[:, pl.ds(0, OWNERS - 1)], self.sent.at[2])

        @pl.when(jnp.logical_not(is_owner(z)))
        def _():
            self.wait_sent(self.to_z, self.sent.at[2])


class Gather:
    def __init__(self, refs):
        self.full, self.rz, self.ry, self.rc, self.sent = refs

    def chunk(self, kind, cc, yy):
        return self.full.at[kind, cc, yy]

    def over_z(self, kind, shard):
        y, z, core = place()
        self.full[kind, core, y, z - OWN_LO] = shard.astype(BF)
        self.send_z(kind)

    def send_z(self, kind):
        y, z, core = place()
        src = self.full.at[kind, core, y, z - OWN_LO]
        for off in (4, 3, 5, 2, 6, 1, 7):
            remote(
                src, src, self.sent.at[0], self.rz.at[kind, z - OWN_LO], turn=turn_of(y, lax.rem(z + off, NZ), core)
            ).start()

    def wait(self, ref, sem):
        y, z, core = place()
        remote(ref, ref, sem, sem, turn=turn_of(y, z, 1 - core)).wait_recv()

    def wait_sent(self, ref, sem):
        y, z, core = place()
        remote(ref, ref, sem, sem, turn=turn_of(y, z, 1 - core)).wait_send()

    def over_y(self, kind):
        y, z, core = place()
        for step in range(OWNERS):
            owner = nearest(z, step)

            @pl.when(z != owner + OWN_LO)
            def _(owner=owner):
                self.wait(self.full.at[kind, core, y, owner], self.rz.at[kind, owner])

            src = self.full.at[kind, core, y, owner]
            self.spread_y(kind, src)
            remote(src, src, self.sent.at[2], self.rc.at[kind, 0], turn=turn_of(y, z, 1 - core)).start()

    def spread_y(self, kind, src):
        y, z, core = place()
        for off in Y_ORDER:
            remote(src, src, self.sent.at[1], self.ry.at[kind, off], turn=turn_of(lax.rem(y + off, NY), z, core)).start()

    def over_core(self, kind, off):
        y, z, core = place()
        chunk = self.chunk(kind, core, lax.rem(y + NY - off, NY))
        self.wait(chunk, self.ry.at[kind, off])
        remote(chunk, chunk, self.sent.at[2], self.rc.at[kind, off], turn=turn_of(y, z, 1 - core)).start()

    def last(self, kind, off):
        y, z, core = place()
        self.wait(self.chunk(kind, 1 - core, lax.rem(y + NY - off, NY)), self.rc.at[kind, off])

    def finish(self, shards, chunks):
        y, z, core = place()

        @pl.when(is_owner(z))
        def _():
            self.wait_sent(shards, self.sent.at[0])

        self.wait_sent(chunks, self.sent.at[1])
        self.wait_sent(self.full.at[:, 0], self.sent.at[2])


class Foreign(Gather):
    def __init__(self, refs):
        self.full, self.rz, self.ry, self.sent = refs

    def chunk(self, kind, cc, yy):
        return self.full.at[kind, yy]

    def over_z(self, kind, src, head):
        y, z, core = place()
        for off in (0, 1, 7, 2, 6, 3, 5, 4):
            remote(
                src, self.full.at[kind, y, z - OWN_LO], self.sent.at[0], self.rz.at[kind, z - OWN_LO],
                turn=turn_of(y, lax.rem(z + off, NZ), core), head=head,
            ).start()

    def over_y(self, kind):
        y, z, core = place()
        for step in reversed(range(OWNERS)):
            owner = nearest(z, step)
            src = self.full.at[kind, y, owner]
            self.wait(src, self.rz.at[kind, owner])
            self.spread_y(kind, src)

    def arrived(self, kind, off):
        y, z, core = place()
        self.wait(self.chunk(kind, core, lax.rem(y + NY - off, NY)), self.ry.at[kind, off])


def inverse_rms(values):
    return lax.rsqrt(jnp.mean(values * values, axis=-1, keepdims=True) + EPS)


def rows_dot(a, b):
    return lax.dot_general(a, b, (((1,), (1,)), ((), ())), preferred_element_type=F32)


def columns_dot(a, b):
    return lax.dot_general(a, b, (((0,), (0,)), ((), ())), preferred_element_type=F32)


def cross_kernel(
    tile_turn_in, tile_len_in, query, grad_out, vision_in, w_key_in, w_value_in, text_turn_in, q_gain_in, k_gain_in,
    att_buf, gq_buf, grad_vision, grad_w_key, grad_w_value,
    q_buf, up_buf, vision, w_key, w_value, text_turn, q_gain, k_gain, tile_turn, tile_len, s_io, qa, da, ka, va, inv, expo, slot_grad,
    weights_kv, vision_t, v_terms, to_c, own, raw, d_kv, to_x, from_x, near_weights, far_weights, sx, sn, sw, edge, beside, ready, *scratch
):
    y, z, core = place()
    head = lax.axis_index("head")
    hi, x = head // NX, lax.rem(head, NX)
    rows, heads = q_buf.shape[0], q_buf.shape[1] // HD
    far_head = (1 - hi) * NX + x
    low, high = z == 0, z == NZ - 1
    at_edge = jnp.logical_or(low, high)
    my_edge = (z // (NZ // 2)) * (NZ - 1)

    barrier = pltpu.get_barrier_semaphore()

    def greet(**peer):
        pl.semaphore_signal(barrier, inc=1, device_id=peer, device_id_type=MESH)

    x_peers = [hi * NX + lax.rem(x + off, NX) for off in range(1, NX)]

    @pl.when(at_edge)
    def _():
        greet(turn=turn_of(y, NZ - 1 - z, core), head=far_head)

    @pl.when(jnp.logical_not(at_edge))
    def _():
        greet(turn=turn_of(y, my_edge, core))

    @pl.when(is_owner(z))
    def _():
        for off in range(1, NZ):
            greet(turn=turn_of(y, lax.rem(z + off, NZ), core))

    @pl.when(jnp.logical_not(is_owner(z)))
    def _():
        for owner in range(OWNERS):
            greet(turn=turn_of(y, owner + OWN_LO, core))

    for off in range(1, NY):
        greet(turn=turn_of(lax.rem(y + off, NY), z, core))

    @pl.when(z == OWN_LO)
    def _():
        for peer in x_peers:
            greet(head=peer)

    greet(turn=turn_of(y, z, 1 - core))

    loads = [
        pltpu.make_async_copy(src, dst, s_io.at[n])
        for n, (src, dst) in enumerate(
            (
                (vision_in, vision), (w_key_in, w_key), (w_value_in, w_value), (tile_turn_in, tile_turn), (tile_len_in, tile_len),
                (text_turn_in, text_turn), (q_gain_in, q_gain), (k_gain_in, k_gain), (query, q_buf), (grad_out, up_buf),
            )
        )
    ]
    for load in loads:
        load.start()

    def columns(h):
        return slice(None), pl.ds(pl.multiple_of(h * HD, HD), HD)

    for load in loads[:3]:
        load.wait()
    weights_kv[:, :HD] = w_key[...]
    weights_kv[:, HD:] = w_value[...]

    def project(cc, out):
        both = jnp.dot(vision[cc].reshape(NY * CHUNK, vision.shape[-1]), weights_kv[...], preferred_element_type=F32)
        for kind in range(2):
            out[kind] = both[:, kind * HD : (kind + 1) * HD].reshape(NY, CHUNK, HD).astype(out.dtype)

    project(1 - core, to_c)
    project(core, own)

    def norm_queries(h, carry):
        gain_q = q_gain[...]
        q_float = q_buf[columns(h)].astype(F32)
        inverse = inverse_rms(q_float)
        inv[h] = inverse
        qa[h, :, :HD] = (q_float * inverse * (gain_q * (SCALE * LOG2E))).astype(BF)
        return carry

    common = 1 + (NY - 1)
    ends = NZ // 2 - 1 + 1
    owner = is_owner(z)
    for here, count in (
        (z == OWN_LO, NZ - 1 + NX - 1),
        (jnp.logical_and(owner, z != OWN_LO), NZ - 1),
        (at_edge, OWNERS + ends),
        (jnp.logical_not(jnp.logical_or(owner, at_edge)), OWNERS),
    ):

        @pl.when(here)
        def _(count=count):
            pl.semaphore_wait(barrier, common + count)

    @pl.when(at_edge)
    def _():
        pl.semaphore_signal(
            edge, inc=1, device_id={"turn": turn_of(y, NZ - 1 - z, core), "head": far_head}, device_id_type=MESH
        )

    @pl.when(z == OWN_LO)
    def _():
        for peer in x_peers:
            pl.semaphore_signal(beside, inc=1, device_id={"head": peer}, device_id_type=MESH)

    scatter = Scatter(scratch[:10], lambda kind, yy: to_c.at[kind, yy], lambda kind, yy: own[kind, yy])
    gather = Gather(scratch[10:15])
    for kind in range(2):
        for off in Y_ORDER + (0,):
            scatter.core_copy(kind, off).start()
    for kind, weight in enumerate((w_key, w_value)):
        near_weights[kind, 0] = weight[...]
        remote(weight, near_weights.at[kind, 1], sn.at[0], sn.at[1], turn=turn_of(y, z, 1 - core)).start()
    scatter.over_core(0)
    scatter.over_core(1)
    for load in loads[3:]:
        load.wait()
    for tile in range(SLOTS // TILE_TOK):
        inside = lax.broadcasted_iota(jnp.int32, (TILE_TOK, HD), 0)
        turn = lax.broadcasted_iota(jnp.int32, (TILE_TOK, HD), 1)
        shown = jnp.where(inside < tile_len[tile], tile_turn[tile], TURNS)
        hidden = jnp.logical_and(shown > turn, turn < TURNS)
        ka[pl.ds(tile * TILE_TOK, TILE_TOK), HD:] = jnp.where(hidden, MASKED, 0.0).astype(BF)
    va[:, HD:] = jnp.ones((SLOTS, HD), BF)
    vision_t[...] = vision[...].reshape(SLOTS, vision.shape[-1]).T
    for part in range(rows // HD):
        turn = lax.broadcasted_iota(jnp.int32, (HD, HD), 0)
        chosen = jnp.where(turn == text_turn[pl.ds(part, 1), :], 1.0, 0.0).T.astype(BF)
        for h in range(heads):
            qa[h, pl.ds(part * HD, HD), HD:] = chosen

    lax.fori_loop(0, 3, norm_queries, 0)
    scatter.over_y(0)
    lax.fori_loop(3, heads, norm_queries, 0)
    scatter.over_y(1)

    def key_shard(total):
        raw[...] = total
        gather.over_z(0, total * inverse_rms(total) * k_gain[...])

    scatter.over_z(0, key_shard)
    gather.over_y(0)
    scatter.over_z(1, lambda total: gather.over_z(1, total))
    for off in Y_ARRIVAL:
        gather.over_core(0, off)
    gather.over_y(1)
    for off in range(NY):
        gather.last(0, off)
    ka[:, :HD] = gather.full[0].reshape(SLOTS, HD)

    def score(h):
        expo[h] = jnp.exp2(rows_dot(qa[h], ka[...])).astype(BF)

    def score_pair(pair, carry):
        score(2 * pair)
        score(2 * pair + 1)

        @pl.when(pair == 1)
        def _():
            for off in Y_ARRIVAL:
                gather.over_core(1, off)

        return carry

    lax.fori_loop(0, heads // 2, score_pair, 0)
    for off in range(NY):
        gather.last(1, off)

    @pl.when(z == OWN_LO)
    def _():
        pl.semaphore_wait(beside, NX - 1)

    @pl.when(at_edge)
    def _():
        pl.semaphore_wait(edge, 1)

    @pl.when(jnp.logical_or(z == OWN_LO, at_edge))
    def _():
        pl.semaphore_signal(ready, inc=1)
        for off in range(1, NZ):
            pl.semaphore_signal(
                ready, inc=1, device_id={"turn": turn_of(y, lax.rem(z + off, NZ), core)}, device_id_type=MESH
            )

    va[:, :HD] = gather.full[1].reshape(SLOTS, HD)

    lane = lax.broadcasted_iota(jnp.int32, (rows, HD), 1)
    slot_grad[...] = jnp.zeros_like(slot_grad)

    def forward(h):
        weights = expo[h]
        summed = jnp.dot(weights, va[...], preferred_element_type=F32)
        over = 1.0 / summed[:, HD:]
        att = (summed[:, :HD] * over).astype(BF)
        att_buf[columns(h)] = att
        up = up_buf[columns(h)].astype(F32)
        delta = -jnp.sum(up * att.astype(F32), axis=1, keepdims=True) * over
        high = delta.astype(BF)
        low = (delta - high.astype(F32)).astype(BF)
        up = (up * over).astype(BF)
        da[h, :, :HD] = up
        da[h, :, HD:] = jnp.where(lane == 0, high, jnp.where(lane == 1, low, jnp.zeros_like(low)))
        slot_grad[1] += columns_dot(up, weights)

    def forward_pair(pair, carry):
        for one in range(4):
            forward(4 * pair + one)
        return carry

    lax.fori_loop(0, heads // 4, forward_pair, 0)

    sums = Scatter(
        scratch[15:25], lambda kind, yy: d_kv.at[kind, 1 - core, yy], lambda kind, yy: d_kv[kind, core, yy]
    )
    back = Gather(scratch[25:30])
    far = Foreign(scratch[30:35])

    def put(kind, factor):
        for cc in (1 - core, core):
            for off in Y_ORDER + (0,):
                yy = lax.rem(y + off, NY)
                start = pl.multiple_of((cc * NY + yy) * CHUNK, CHUNK)
                d_kv[kind, cc, yy] = (slot_grad[kind, :, pl.ds(start, CHUNK)] * factor).T.astype(BF)
                if cc is not core:
                    sums.core_copy(kind, off).start()

    put(1, 1.0)
    pl.semaphore_wait(ready, 3)
    from_core = near_weights.at[:, 1]
    remote(from_core, from_core, sn.at[0], sn.at[1], turn=turn_of(y, z, 1 - core)).wait()

    direct, relayed = core == hi, core != hi

    @pl.when(relayed)
    def _():
        for kind in range(2):
            remote(near_weights.at[kind], far_weights.at[kind], sw.at[0], sw.at[1], head=far_head).start()

    def backward(h):
        d_scores = expo[h] * rows_dot(da[h], va[...]).astype(BF)
        expo[h] = d_scores
        slot_grad[0] += columns_dot(qa[h, :, :HD], d_scores)

    def backward_pair(pair, carry):
        backward(2 * pair)
        backward(2 * pair + 1)

        @pl.when(pair == 0)
        def _():
            sums.over_core(1)

        @pl.when(pair == 3)
        def _():
            sums.over_y(1)

        return carry

    lax.fori_loop(0, heads // 2, backward_pair, 0)
    put(0, 1.0 / LOG2E)

    def spread(kind, total):
        back.full[kind, core, y, z - OWN_LO] = total.astype(BF)

        @pl.when(core != hi)
        def _():
            far.over_z(kind, back.full.at[kind, core, y, z - OWN_LO], far_head)

        back.send_z(kind)

    def query_grad(h):
        d_query = jnp.dot(expo[h], ka[:, :HD], preferred_element_type=F32)
        q_float = q_buf[columns(h)].astype(F32)
        inverse = inv[h]
        scaled = d_query * (q_gain[...] * SCALE)
        gq_buf[columns(h)] = (
            inverse * scaled - q_float * (inverse * inverse * inverse) * jnp.mean(q_float * scaled, axis=1, keepdims=True)
        ).astype(BF)

    def query_pair(pair, carry):
        query_grad(2 * pair)
        query_grad(2 * pair + 1)

        @pl.when(pair == 0)
        def _():
            sums.over_core(0)

        @pl.when(pair == 2)
        def _():
            sums.over_z(1, lambda total: spread(1, total))

        @pl.when(pair == 3)
        def _():
            sums.over_y(0)

        return carry

    lax.fori_loop(0, heads // 2, query_pair, 0)


    def key_grad_shard(total):
        raw_values = raw[...]
        inverse = inverse_rms(raw_values)
        scaled = total * k_gain[...]
        spread(
            0,
            inverse * scaled
            - raw_values * (inverse * inverse * inverse) * jnp.mean(raw_values * scaled, axis=1, keepdims=True),
        )

    sums.over_z(0, key_grad_shard)
    def far_over_y(kind):
        @pl.when(direct)
        def _():
            far.over_y(kind)

    def vision_term(kind, off):
        yy = lax.rem(y + NY - off, NY)
        return rows_dot(
            back.full[kind, hi, yy].reshape(CHUNK, HD), near_weights[kind].reshape(NC * CHUNK, HD)
        ) + rows_dot(far.full[kind, yy].reshape(CHUNK, HD), far_weights[kind].reshape(NC * CHUNK, HD))

    def send_terms(off):
        yy = lax.rem(y + NY - off, NY)
        both = v_terms[off] + vision_term(0, off)
        slot = lax.rem(yy - x + NX + NX - 1, NX)
        width = vision.shape[-1]
        to_x[NC * off] = both[:, :width].astype(BF)
        to_x[NC * off + 1] = both[:, width:].astype(BF)
        remote(
            to_x.at[NC * off + 1], from_x.at[slot], sx.at[0], sx.at[1], turn=turn_of(y, z, 1 - core), head=hi * NX + yy
        ).start()

        @pl.when(yy != x)
        def _():
            remote(to_x.at[NC * off], from_x.at[slot], sx.at[0], sx.at[1], head=hi * NX + yy).start()

    def weight_grad(kind, out):
        out[...] = jnp.dot(vision_t[...], back.full[kind].reshape(SLOTS, HD), preferred_element_type=F32)

    back.over_y(1)
    far_over_y(1)
    back.over_y(0)
    for off in Y_ARRIVAL:
        back.over_core(1, off)

    @pl.when(direct)
    def _():
        remote(far_weights, far_weights, sw.at[0], sw.at[1], head=far_head).wait_recv()
        for off in Y_ARRIVAL:
            far.arrived(1, off)

    far_over_y(0)

    @pl.when(direct)
    def _():
        for off in range(NY):
            v_terms[off] = vision_term(1, off)

    for off in range(NY):
        back.last(1, off)
    weight_grad(1, grad_w_value)

    for off in (0,) + Y_ARRIVAL:
        if off:
            back.over_core(0, off)

        @pl.when(direct)
        def _(off=off):
            if off:
                far.arrived(0, off)
            send_terms(off)

    for off in range(NY):
        back.last(0, off)
    weight_grad(0, grad_w_key)

    scatter.finish()
    sums.finish()
    gather.finish(sums.from_z, sums.from_y)
    back.finish(sums.from_z, sums.from_y)

    @pl.when(direct)
    def _():
        far.wait_sent(sums.from_y, far.sent.at[1])

    @pl.when(relayed)
    def _():
        remote(near_weights, near_weights, sw.at[0], sw.at[1], head=far_head).wait_send()

    @pl.when(jnp.logical_and(relayed, is_owner(z)))
    def _():
        far.wait_sent(back.full.at[:, 0], far.sent.at[0])

    def landed(count):
        part = from_x.at[pl.ds(0, count)]
        remote(part, part, sx.at[0], sx.at[1], head=x_peers[0]).wait_recv()
        total = from_x[0].astype(F32)
        for slot in range(1, count):
            total = total + from_x[slot].astype(F32)
        return total

    @pl.when(direct)
    def _():
        sent = to_x.at[pl.ds(0, NC * NY - 1)]
        remote(sent, sent, sx.at[0], sx.at[1], head=x_peers[0]).wait_send()
        grad_vision[...] = (landed(NX - 1) + to_x[NC * lax.rem(y - x + NY, NY)].astype(F32)).astype(BF)

    @pl.when(relayed)
    def _():
        grad_vision[...] = landed(NX).astype(BF)


def cross(tile_turn, tile_len, query, grad_out, vision, w_key, w_value, text_turn, q_gain, k_gain):
    vmem = pl.BlockSpec(memory_space=pltpu.VMEM)
    hbm = pl.BlockSpec(memory_space=pltpu.HBM)
    rows, columns = query.shape
    heads = columns // HD
    width = vision.shape[1]
    return pl.pallas_call(
        cross_kernel,
        out_shape=(
            jax.ShapeDtypeStruct(query.shape, BF),
            jax.ShapeDtypeStruct(query.shape, BF),
            jax.ShapeDtypeStruct((CHUNK, width), BF),
            jax.ShapeDtypeStruct((width, HD), F32),
            jax.ShapeDtypeStruct((width, HD), F32),
        ),
        in_specs=[hbm] * 10,
        out_specs=(vmem,) * 5,
        scratch_shapes=[
            pltpu.VMEM((rows, columns), BF),
            pltpu.VMEM((rows, columns), BF),
            pltpu.VMEM((NC, NY, CHUNK, width), BF),
            pltpu.VMEM((width, HD), BF),
            pltpu.VMEM((width, HD), BF),
            pltpu.VMEM((rows // HD, HD), jnp.int32),
            pltpu.VMEM((1, HD), F32),
            pltpu.VMEM((1, HD), F32),
            pltpu.SMEM((SLOTS // TILE_TOK,), jnp.int32),
            pltpu.SMEM((SLOTS // TILE_TOK,), jnp.int32),
            pltpu.SemaphoreType.DMA((10,)),
            pltpu.VMEM((heads, rows, 2 * HD), BF),
            pltpu.VMEM((heads, rows, 2 * HD), BF),
            pltpu.VMEM((SLOTS, 2 * HD), BF),
            pltpu.VMEM((SLOTS, 2 * HD), BF),
            pltpu.VMEM((heads, rows, 1), F32),
            pltpu.VMEM((heads, rows, SLOTS), BF),
            pltpu.VMEM((2, HD, SLOTS), F32),
            pltpu.VMEM((HD, 2 * HD), BF),
            pltpu.VMEM((width, SLOTS), BF),
            pltpu.VMEM((NY, CHUNK, NC * width), F32),
            pltpu.VMEM((2, NY, CHUNK, HD), BF),
            pltpu.VMEM((2, NY, CHUNK, HD), F32),
            pltpu.VMEM((SHARD, HD), F32),
            pltpu.VMEM((2, NC, NY, CHUNK, HD), BF),
            pltpu.VMEM((NY * NC, CHUNK, width), BF),
            pltpu.VMEM((NX, CHUNK, width), BF),
            pltpu.VMEM((2, NC, width, HD), BF),
            pltpu.VMEM((2, NC, width, HD), BF),
            pltpu.SemaphoreType.DMA((2,)),
            pltpu.SemaphoreType.DMA((2,)),
            pltpu.SemaphoreType.DMA((2,)),
            pltpu.SemaphoreType.REGULAR,
            pltpu.SemaphoreType.REGULAR,
            pltpu.SemaphoreType.REGULAR,
        ]
        + (scatter_scratch() + gather_scratch()) * 2
        + foreign_scratch(),
        compiler_params=pltpu.CompilerParams(collective_id=0, has_side_effects=True, vmem_limit_bytes=VMEM_LIMIT),
        name="cross",
    )(
        *(
            pltpu.with_memory_space_constraint(operand, pltpu.HBM)
            for operand in (
                tile_turn, tile_len, query, grad_out, vision.reshape(NC, NY, CHUNK, width), w_key, w_value, text_turn,
                q_gain, k_gain,
            )
        )
    )


def emit_kernel(*refs):
    count = len(refs) // 2
    copies = []
    for i in range(count):
        for start in range(0, refs[i].shape[0], CHUNK):
            part = pl.ds(start, CHUNK)
            copies.append(pltpu.make_async_copy(refs[i].at[part], refs[count + i].at[part], refs[-1].at[len(copies)]))
    for copy in copies:
        copy.start()
    for copy in copies:
        copy.wait()


def emit(arrays):
    vmem = pl.BlockSpec(memory_space=pltpu.VMEM)
    hbm = pl.BlockSpec(memory_space=pltpu.HBM)
    return pl.pallas_call(
        emit_kernel,
        out_shape=tuple(jax.ShapeDtypeStruct(a.shape, a.dtype) for a in arrays),
        in_specs=[vmem] * len(arrays),
        out_specs=(hbm,) * len(arrays),
        scratch_shapes=[pltpu.SemaphoreType.DMA((sum(a.shape[0] // CHUNK for a in arrays),))],
        compiler_params=pltpu.CompilerParams(vmem_limit_bytes=8 * 1024 * 1024),
        name="emit",
    )(*arrays)


def body(query, vision, w_key, w_value, q_gain, k_gain, text_turn, tile_turn, tile_len, grad_out):
    outs = cross(
        tile_turn, tile_len, query, grad_out, vision, w_key, w_value,
        text_turn.reshape(-1, HD), q_gain.reshape(1, HD), k_gain.reshape(1, HD),
    )
    return emit(outs)


def solution(mesh):
    return jax.shard_map(
        body,
        mesh=mesh,
        in_specs=(
            P("turn", "head"),
            P(None, "turn"),
            P("turn", "head"),
            P("turn", "head"),
            P(),
            P(),
            P("turn"),
            P(),
            P(),
            P("turn", "head"),
        ),
        out_specs=(
            P("turn", "head"),
            P("turn", "head"),
            P("head", "turn"),
            P("turn", "head"),
            P("turn", "head"),
        ),
        check_vma=False,
    )
```

```python
import math

import jax
import jax.numpy as jnp
from jax import lax
from jax.experimental import pallas as pl
from jax.experimental.pallas import tpu as pltpu
from jax.sharding import PartitionSpec as P

HD = 128
TILE_TOK = 256
TURNS = 64
EPS = 1e-05

NY, NZ, NC = 4, 8, 2
NHI, NX = 2, 4
CHUNK = 128
OWN_LO, OWNERS = 3, 2
SHARD = CHUNK // OWNERS
SLOTS = NC * NY * CHUNK

BF = jnp.bfloat16
F32 = jnp.float32
MESH = pl.DeviceIdType.MESH
SCALE = 1.0 / math.sqrt(HD)
LOG2E = math.log2(math.e)
MASKED = -16384.0
VMEM_LIMIT = 40 * 1024 * 1024

Y_ORDER = (2, 1, 3)
Y_ARRIVAL = (1, 3, 2)


def place():
    turn = lax.axis_index("turn")
    core = lax.rem(turn, NC)
    z = lax.rem(turn // NC, NZ)
    y = turn // (NC * NZ)
    return y, z, core


def turn_of(y, z, core):
    return (y * NZ + z) * NC + core


def is_owner(z):
    return jnp.logical_and(z >= OWN_LO, z < OWN_LO + OWNERS)


def remote(src, dst, send, recv, **where):
    return pltpu.make_async_remote_copy(
        src_ref=src, dst_ref=dst, send_sem=send, recv_sem=recv, device_id=where, device_id_type=MESH
    )


def nearest(z, step):
    far = z // (NZ // 2)
    return step * (1 - far) + (OWNERS - 1 - step) * far


def scatter_scratch():
    return [
        pltpu.VMEM((2, NY, CHUNK, HD), BF),
        pltpu.VMEM((2, NY, OWNERS, SHARD, HD), BF),
        pltpu.VMEM((2, OWNERS, NY - 1, SHARD, HD), BF),
        pltpu.VMEM((2, OWNERS, SHARD, HD), F32),
        pltpu.VMEM((2, OWNERS, SHARD, HD), BF),
        pltpu.VMEM((2, NZ - 1, SHARD, HD), BF),
        pltpu.SemaphoreType.DMA((2, NY)),
        pltpu.SemaphoreType.DMA((2, OWNERS)),
        pltpu.SemaphoreType.DMA((2,)),
        pltpu.SemaphoreType.DMA((3,)),
    ]


def gather_scratch():
    return [
        pltpu.VMEM((2, NC, NY, OWNERS, SHARD, HD), BF),
        pltpu.SemaphoreType.DMA((2, OWNERS)),
        pltpu.SemaphoreType.DMA((2, NY)),
        pltpu.SemaphoreType.DMA((2, NY)),
        pltpu.SemaphoreType.DMA((3,)),
    ]


def foreign_scratch():
    return [
        pltpu.VMEM((2, NY, OWNERS, SHARD, HD), BF),
        pltpu.SemaphoreType.DMA((2, OWNERS)),
        pltpu.SemaphoreType.DMA((2, NY)),
        pltpu.SemaphoreType.DMA((2,)),
    ]


class Scatter:
    def __init__(self, refs, source, own):
        (self.from_c, self.to_y, self.from_y, self.total, self.to_z, self.from_z, self.rc, self.ry, self.rz, self.sent) = refs
        self.source = source
        self.own = own

    def core_copy(self, kind, off):
        y, z, core = place()
        yy = lax.rem(y + off, NY)
        return remote(
            self.source(kind, yy), self.from_c.at[kind, yy], self.sent.at[0], self.rc.at[kind, off],
            turn=turn_of(y, z, 1 - core),
        )

    def over_core(self, kind):
        y, z, core = place()
        for off in Y_ORDER + (0,):
            yy = lax.rem(y + off, NY)
            self.core_copy(kind, off).wait_recv()
            both = self.own(kind, yy).astype(F32) + self.from_c[kind, yy].astype(F32)
            both = both.reshape(OWNERS, SHARD, HD)
            if off == 0:
                self.total[kind] = both
            else:
                self.to_y[kind, off] = both.astype(BF)
        for step in reversed(range(OWNERS)):
            owner = nearest(z, step)
            for off in Y_ORDER:
                remote(
                    self.to_y.at[kind, off, owner], self.from_y.at[kind, owner, off - 1], self.sent.at[1],
                    self.ry.at[kind, owner], turn=turn_of(lax.rem(y + off, NY), z, core),
                ).start()

    def wait(self, ref, sem):
        y, z, core = place()
        remote(ref, ref, sem, sem, turn=turn_of(y, z, 1 - core)).wait_recv()

    def wait_sent(self, ref, sem):
        y, z, core = place()
        remote(ref, ref, sem, sem, turn=turn_of(y, z, 1 - core)).wait_send()

    def over_y(self, kind):
        y, z, core = place()
        for step in reversed(range(OWNERS)):
            owner = nearest(z, step)
            self.wait(self.from_y.at[kind, owner], self.ry.at[kind, owner])
            total = self.total[kind, owner]
            for off in range(1, NY):
                total = total + self.from_y[kind, owner, off - 1].astype(F32)
            self.total[kind, owner] = total
            self.to_z[kind, owner] = total.astype(BF)

            @pl.when(owner + OWN_LO != z)
            def _(owner=owner):
                slot = lax.rem(z - owner - OWN_LO + NZ + NZ - 1, NZ)
                remote(
                    self.to_z.at[kind, owner], self.from_z.at[kind, slot], self.sent.at[2], self.rz.at[kind],
                    turn=turn_of(y, owner + OWN_LO, core),
                ).start()

    def over_z(self, kind, then):
        y, z, core = place()

        @pl.when(is_owner(z))
        def _():
            total = self.total[kind, z - OWN_LO]
            self.wait(self.from_z.at[kind], self.rz.at[kind])
            for slot in range(NZ - 1):
                total = total + self.from_z[kind, slot].astype(F32)
            then(total)

    def finish(self):
        y, z, core = place()
        self.wait_sent(self.from_c, self.sent.at[0])
        self.wait_sent(self.from_y, self.sent.at[1])

        @pl.when(is_owner(z))
        def _():
            self.wait_sent(self.to_z.at[:, pl.ds(0, OWNERS - 1)], self.sent.at[2])

        @pl.when(jnp.logical_not(is_owner(z)))
        def _():
            self.wait_sent(self.to_z, self.sent.at[2])


class Gather:
    def __init__(self, refs):
        self.full, self.rz, self.ry, self.rc, self.sent = refs

    def chunk(self, kind, cc, yy):
        return self.full.at[kind, cc, yy]

    def over_z(self, kind, shard):
        y, z, core = place()
        self.full[kind, core, y, z - OWN_LO] = shard.astype(BF)
        self.send_z(kind)

    def send_z(self, kind):
        y, z, core = place()
        src = self.full.at[kind, core, y, z - OWN_LO]
        for off in (4, 3, 5, 2, 6, 1, 7):
            remote(
                src, src, self.sent.at[0], self.rz.at[kind, z - OWN_LO], turn=turn_of(y, lax.rem(z + off, NZ), core)
            ).start()

    def wait(self, ref, sem):
        y, z, core = place()
        remote(ref, ref, sem, sem, turn=turn_of(y, z, 1 - core)).wait_recv()

    def wait_sent(self, ref, sem):
        y, z, core = place()
        remote(ref, ref, sem, sem, turn=turn_of(y, z, 1 - core)).wait_send()

    def over_y(self, kind):
        y, z, core = place()
        for step in range(OWNERS):
            owner = nearest(z, step)

            @pl.when(z != owner + OWN_LO)
            def _(owner=owner):
                self.wait(self.full.at[kind, core, y, owner], self.rz.at[kind, owner])

            src = self.full.at[kind, core, y, owner]
            self.spread_y(kind, src)
            remote(src, src, self.sent.at[2], self.rc.at[kind, 0], turn=turn_of(y, z, 1 - core)).start()

    def spread_y(self, kind, src):
        y, z, core = place()
        for off in Y_ORDER:
            remote(src, src, self.sent.at[1], self.ry.at[kind, off], turn=turn_of(lax.rem(y + off, NY), z, core)).start()

    def over_core(self, kind, off):
        y, z, core = place()
        chunk = self.chunk(kind, core, lax.rem(y + NY - off, NY))
        self.wait(chunk, self.ry.at[kind, off])
        remote(chunk, chunk, self.sent.at[2], self.rc.at[kind, off], turn=turn_of(y, z, 1 - core)).start()

    def last(self, kind, off):
        y, z, core = place()
        self.wait(self.chunk(kind, 1 - core, lax.rem(y + NY - off, NY)), self.rc.at[kind, off])

    def finish(self, shards, chunks):
        y, z, core = place()

        @pl.when(is_owner(z))
        def _():
            self.wait_sent(shards, self.sent.at[0])

        self.wait_sent(chunks, self.sent.at[1])
        self.wait_sent(self.full.at[:, 0], self.sent.at[2])


class Foreign(Gather):
    def __init__(self, refs):
        self.full, self.rz, self.ry, self.sent = refs

    def chunk(self, kind, cc, yy):
        return self.full.at[kind, yy]

    def over_z(self, kind, src, head):
        y, z, core = place()
        for off in (0, 1, 7, 2, 6, 3, 5, 4):
            remote(
                src, self.full.at[kind, y, z - OWN_LO], self.sent.at[0], self.rz.at[kind, z - OWN_LO],
                turn=turn_of(y, lax.rem(z + off, NZ), core), head=head,
            ).start()

    def over_y(self, kind):
        y, z, core = place()
        for step in reversed(range(OWNERS)):
            owner = nearest(z, step)
            src = self.full.at[kind, y, owner]
            self.wait(src, self.rz.at[kind, owner])
            self.spread_y(kind, src)

    def arrived(self, kind, off):
        y, z, core = place()
        self.wait(self.chunk(kind, core, lax.rem(y + NY - off, NY)), self.ry.at[kind, off])


def inverse_rms(values):
    return lax.rsqrt(jnp.mean(values * values, axis=-1, keepdims=True) + EPS)


def rows_dot(a, b):
    return lax.dot_general(a, b, (((1,), (1,)), ((), ())), preferred_element_type=F32)


def columns_dot(a, b):
    return lax.dot_general(a, b, (((0,), (0,)), ((), ())), preferred_element_type=F32)


def cross_kernel(
    tile_turn_in, tile_len_in, query, grad_out, vision_in, w_key_in, w_value_in, text_turn_in, q_gain_in, k_gain_in,
    att_buf, gq_buf, grad_vision, grad_w_key, grad_w_value,
    q_buf, up_buf, vision, w_key, w_value, text_turn, q_gain, k_gain, tile_turn, tile_len, s_io, qa, da, ka, va, inv, expo, slot_grad,
    weights_kv, vision_t, v_terms, to_c, own, raw, d_kv, to_x, from_x, near_weights, far_weights, sx, sn, sw, edge, beside, ready, *scratch
):
    y, z, core = place()
    head = lax.axis_index("head")
    hi, x = head // NX, lax.rem(head, NX)
    rows, heads = q_buf.shape[0], q_buf.shape[1] // HD
    far_head = (1 - hi) * NX + x
    low, high = z == 0, z == NZ - 1
    at_edge = jnp.logical_or(low, high)
    my_edge = (z // (NZ // 2)) * (NZ - 1)

    barrier = pltpu.get_barrier_semaphore()

    def greet(**peer):
        pl.semaphore_signal(barrier, inc=1, device_id=peer, device_id_type=MESH)

    x_peers = [hi * NX + lax.rem(x + off, NX) for off in range(1, NX)]

    @pl.when(at_edge)
    def _():
        greet(turn=turn_of(y, NZ - 1 - z, core), head=far_head)

    @pl.when(jnp.logical_not(at_edge))
    def _():
        greet(turn=turn_of(y, my_edge, core))

    @pl.when(is_owner(z))
    def _():
        for off in range(1, NZ):
            greet(turn=turn_of(y, lax.rem(z + off, NZ), core))

    @pl.when(jnp.logical_not(is_owner(z)))
    def _():
        for owner in range(OWNERS):
            greet(turn=turn_of(y, owner + OWN_LO, core))

    for off in range(1, NY):
        greet(turn=turn_of(lax.rem(y + off, NY), z, core))

    @pl.when(z == OWN_LO)
    def _():
        for peer in x_peers:
            greet(head=peer)

    greet(turn=turn_of(y, z, 1 - core))

    loads = [
        pltpu.make_async_copy(src, dst, s_io.at[n])
        for n, (src, dst) in enumerate(
            (
                (vision_in, vision), (w_key_in, w_key), (w_value_in, w_value), (tile_turn_in, tile_turn), (tile_len_in, tile_len),
                (text_turn_in, text_turn), (q_gain_in, q_gain), (k_gain_in, k_gain), (query, q_buf), (grad_out, up_buf),
            )
        )
    ]
    for load in loads:
        load.start()

    def columns(h):
        return slice(None), pl.ds(pl.multiple_of(h * HD, HD), HD)

    for load in loads[:3]:
        load.wait()
    weights_kv[:, :HD] = w_key[...]
    weights_kv[:, HD:] = w_value[...]

    def project(cc, out):
        both = jnp.dot(vision[cc].reshape(NY * CHUNK, vision.shape[-1]), weights_kv[...], preferred_element_type=F32)
        for kind in range(2):
            out[kind] = both[:, kind * HD : (kind + 1) * HD].reshape(NY, CHUNK, HD).astype(out.dtype)

    project(1 - core, to_c)
    project(core, own)

    def norm_queries(h, carry):
        gain_q = q_gain[...]
        q_float = q_buf[columns(h)].astype(F32)
        inverse = inverse_rms(q_float)
        inv[h] = inverse
        qa[h, :, :HD] = (q_float * inverse * (gain_q * (SCALE * LOG2E))).astype(BF)
        return carry

    common = 1 + (NY - 1)
    ends = NZ // 2 - 1 + 1
    owner = is_owner(z)
    for here, count in (
        (z == OWN_LO, NZ - 1 + NX - 1),
        (jnp.logical_and(owner, z != OWN_LO), NZ - 1),
        (at_edge, OWNERS + ends),
        (jnp.logical_not(jnp.logical_or(owner, at_edge)), OWNERS),
    ):

        @pl.when(here)
        def _(count=count):
            pl.semaphore_wait(barrier, common + count)

    @pl.when(at_edge)
    def _():
        pl.semaphore_signal(
            edge, inc=1, device_id={"turn": turn_of(y, NZ - 1 - z, core), "head": far_head}, device_id_type=MESH
        )

    @pl.when(z == OWN_LO)
    def _():
        for peer in x_peers:
            pl.semaphore_signal(beside, inc=1, device_id={"head": peer}, device_id_type=MESH)

    scatter = Scatter(scratch[:10], lambda kind, yy: to_c.at[kind, yy], lambda kind, yy: own[kind, yy])
    gather = Gather(scratch[10:15])
    for kind in range(2):
        for off in Y_ORDER + (0,):
            scatter.core_copy(kind, off).start()
    for kind, weight in enumerate((w_key, w_value)):
        near_weights[kind, 0] = weight[...]
        remote(weight, near_weights.at[kind, 1], sn.at[0], sn.at[1], turn=turn_of(y, z, 1 - core)).start()
    scatter.over_core(0)
    scatter.over_core(1)
    for load in loads[3:]:
        load.wait()
    for tile in range(SLOTS // TILE_TOK):
        inside = lax.broadcasted_iota(jnp.int32, (TILE_TOK, HD), 0)
        turn = lax.broadcasted_iota(jnp.int32, (TILE_TOK, HD), 1)
        shown = jnp.where(inside < tile_len[tile], tile_turn[tile], TURNS)
        hidden = jnp.logical_and(shown > turn, turn < TURNS)
        ka[pl.ds(tile * TILE_TOK, TILE_TOK), HD:] = jnp.where(hidden, MASKED, 0.0).astype(BF)
    va[:, HD:] = jnp.ones((SLOTS, HD), BF)
    vision_t[...] = vision[...].reshape(SLOTS, vision.shape[-1]).T
    for part in range(rows // HD):
        turn = lax.broadcasted_iota(jnp.int32, (HD, HD), 0)
        chosen = jnp.where(turn == text_turn[pl.ds(part, 1), :], 1.0, 0.0).T.astype(BF)
        for h in range(heads):
            qa[h, pl.ds(part * HD, HD), HD:] = chosen

    lax.fori_loop(0, 3, norm_queries, 0)
    scatter.over_y(0)
    lax.fori_loop(3, heads, norm_queries, 0)
    scatter.over_y(1)

    def key_shard(total):
        raw[...] = total
        gather.over_z(0, total * inverse_rms(total) * k_gain[...])

    scatter.over_z(0, key_shard)
    gather.over_y(0)
    scatter.over_z(1, lambda total: gather.over_z(1, total))
    for off in Y_ARRIVAL:
        gather.over_core(0, off)
    gather.over_y(1)
    for off in range(NY):
        gather.last(0, off)
    ka[:, :HD] = gather.full[0].reshape(SLOTS, HD)

    def score(h):
        expo[h] = jnp.exp2(rows_dot(qa[h], ka[...])).astype(BF)

    def score_pair(pair, carry):
        score(2 * pair)
        score(2 * pair + 1)

        @pl.when(pair == 2)
        def _():
            for off in Y_ARRIVAL:
                gather.over_core(1, off)

        return carry

    lax.fori_loop(0, heads // 2, score_pair, 0)
    for off in range(NY):
        gather.last(1, off)

    @pl.when(z == OWN_LO)
    def _():
        pl.semaphore_wait(beside, NX - 1)

    @pl.when(at_edge)
    def _():
        pl.semaphore_wait(edge, 1)

    @pl.when(jnp.logical_or(z == OWN_LO, at_edge))
    def _():
        pl.semaphore_signal(ready, inc=1)
        for off in range(1, NZ):
            pl.semaphore_signal(
                ready, inc=1, device_id={"turn": turn_of(y, lax.rem(z + off, NZ), core)}, device_id_type=MESH
            )

    va[:, :HD] = gather.full[1].reshape(SLOTS, HD)

    lane = lax.broadcasted_iota(jnp.int32, (rows, HD), 1)
    slot_grad[...] = jnp.zeros_like(slot_grad)

    def forward(h):
        weights = expo[h]
        summed = jnp.dot(weights, va[...], preferred_element_type=F32)
        over = 1.0 / summed[:, HD:]
        att = (summed[:, :HD] * over).astype(BF)
        att_buf[columns(h)] = att
        up = up_buf[columns(h)].astype(F32)
        delta = -jnp.sum(up * att.astype(F32), axis=1, keepdims=True) * over
        high = delta.astype(BF)
        low = (delta - high.astype(F32)).astype(BF)
        up = (up * over).astype(BF)
        da[h, :, :HD] = up
        da[h, :, HD:] = jnp.where(lane == 0, high, jnp.where(lane == 1, low, jnp.zeros_like(low)))
        slot_grad[1] += columns_dot(up, weights)

    def forward_pair(pair, carry):
        for one in range(4):
            forward(4 * pair + one)
        return carry

    lax.fori_loop(0, heads // 4, forward_pair, 0)

    sums = Scatter(
        scratch[15:25], lambda kind, yy: d_kv.at[kind, 1 - core, yy], lambda kind, yy: d_kv[kind, core, yy]
    )
    back = Gather(scratch[25:30])
    far = Foreign(scratch[30:35])

    def put(kind, factor):
        for cc in (1 - core, core):
            for off in Y_ORDER + (0,):
                yy = lax.rem(y + off, NY)
                start = pl.multiple_of((cc * NY + yy) * CHUNK, CHUNK)
                d_kv[kind, cc, yy] = (slot_grad[kind, :, pl.ds(start, CHUNK)] * factor).T.astype(BF)
                if cc is not core:
                    sums.core_copy(kind, off).start()

    put(1, 1.0)
    pl.semaphore_wait(ready, 3)
    from_core = near_weights.at[:, 1]
    remote(from_core, from_core, sn.at[0], sn.at[1], turn=turn_of(y, z, 1 - core)).wait()

    direct, relayed = core == hi, core != hi

    @pl.when(relayed)
    def _():
        for kind in range(2):
            remote(near_weights.at[kind], far_weights.at[kind], sw.at[0], sw.at[1], head=far_head).start()

    def backward(h):
        d_scores = expo[h] * rows_dot(da[h], va[...]).astype(BF)
        expo[h] = d_scores
        slot_grad[0] += columns_dot(qa[h, :, :HD], d_scores)

    def backward_pair(pair, carry):
        backward(2 * pair)
        backward(2 * pair + 1)

        @pl.when(pair == 0)
        def _():
            sums.over_core(1)

        @pl.when(pair == 3)
        def _():
            sums.over_y(1)

        return carry

    lax.fori_loop(0, heads // 2, backward_pair, 0)
    put(0, 1.0 / LOG2E)

    def spread(kind, total):
        back.full[kind, core, y, z - OWN_LO] = total.astype(BF)

        @pl.when(core != hi)
        def _():
            far.over_z(kind, back.full.at[kind, core, y, z - OWN_LO], far_head)

        back.send_z(kind)

    def query_grad(h):
        d_query = jnp.dot(expo[h], ka[:, :HD], preferred_element_type=F32)
        q_float = q_buf[columns(h)].astype(F32)
        inverse = inv[h]
        scaled = d_query * (q_gain[...] * SCALE)
        gq_buf[columns(h)] = (
            inverse * scaled - q_float * (inverse * inverse * inverse) * jnp.mean(q_float * scaled, axis=1, keepdims=True)
        ).astype(BF)

    def query_pair(pair, carry):
        query_grad(2 * pair)
        query_grad(2 * pair + 1)

        @pl.when(pair == 0)
        def _():
            sums.over_core(0)

        @pl.when(pair == 3)
        def _():
            sums.over_y(0)

        return carry

    lax.fori_loop(0, heads // 2, query_pair, 0)


    def key_grad_shard(total):
        raw_values = raw[...]
        inverse = inverse_rms(raw_values)
        scaled = total * k_gain[...]
        spread(
            0,
            inverse * scaled
            - raw_values * (inverse * inverse * inverse) * jnp.mean(raw_values * scaled, axis=1, keepdims=True),
        )

    sums.over_z(1, lambda total: spread(1, total))
    sums.over_z(0, key_grad_shard)
    def far_over_y(kind):
        @pl.when(direct)
        def _():
            far.over_y(kind)

    def vision_term(kind, off):
        yy = lax.rem(y + NY - off, NY)
        return rows_dot(
            back.full[kind, hi, yy].reshape(CHUNK, HD), near_weights[kind].reshape(NC * CHUNK, HD)
        ) + rows_dot(far.full[kind, yy].reshape(CHUNK, HD), far_weights[kind].reshape(NC * CHUNK, HD))

    def send_terms(off):
        yy = lax.rem(y + NY - off, NY)
        both = v_terms[off] + vision_term(0, off)
        slot = lax.rem(yy - x + NX + NX - 1, NX)
        width = vision.shape[-1]
        to_x[NC * off] = both[:, :width].astype(BF)
        to_x[NC * off + 1] = both[:, width:].astype(BF)
        remote(
            to_x.at[NC * off + 1], from_x.at[slot], sx.at[0], sx.at[1], turn=turn_of(y, z, 1 - core), head=hi * NX + yy
        ).start()

        @pl.when(yy != x)
        def _():
            remote(to_x.at[NC * off], from_x.at[slot], sx.at[0], sx.at[1], head=hi * NX + yy).start()

    def weight_grad(kind, out):
        out[...] = jnp.dot(vision_t[...], back.full[kind].reshape(SLOTS, HD), preferred_element_type=F32)

    back.over_y(1)
    far_over_y(1)
    back.over_y(0)
    for off in Y_ARRIVAL:
        back.over_core(1, off)

    @pl.when(direct)
    def _():
        remote(far_weights, far_weights, sw.at[0], sw.at[1], head=far_head).wait_recv()
        for off in Y_ARRIVAL:
            far.arrived(1, off)

    far_over_y(0)

    @pl.when(direct)
    def _():
        for off in range(NY):
            v_terms[off] = vision_term(1, off)

    for off in range(NY):
        back.last(1, off)
    weight_grad(1, grad_w_value)

    for off in (0,) + Y_ARRIVAL:
        if off:
            back.over_core(0, off)

        @pl.when(direct)
        def _(off=off):
            if off:
                far.arrived(0, off)
            send_terms(off)

    for off in range(NY):
        back.last(0, off)
    weight_grad(0, grad_w_key)

    scatter.finish()
    sums.finish()
    gather.finish(sums.from_z, sums.from_y)
    back.finish(sums.from_z, sums.from_y)

    @pl.when(direct)
    def _():
        far.wait_sent(sums.from_y, far.sent.at[1])

    @pl.when(relayed)
    def _():
        remote(near_weights, near_weights, sw.at[0], sw.at[1], head=far_head).wait_send()

    @pl.when(jnp.logical_and(relayed, is_owner(z)))
    def _():
        far.wait_sent(back.full.at[:, 0], far.sent.at[0])

    def landed(count):
        part = from_x.at[pl.ds(0, count)]
        remote(part, part, sx.at[0], sx.at[1], head=x_peers[0]).wait_recv()
        total = from_x[0].astype(F32)
        for slot in range(1, count):
            total = total + from_x[slot].astype(F32)
        return total

    @pl.when(direct)
    def _():
        sent = to_x.at[pl.ds(0, NC * NY - 1)]
        remote(sent, sent, sx.at[0], sx.at[1], head=x_peers[0]).wait_send()
        grad_vision[...] = (landed(NX - 1) + to_x[NC * lax.rem(y - x + NY, NY)].astype(F32)).astype(BF)

    @pl.when(relayed)
    def _():
        grad_vision[...] = landed(NX).astype(BF)


def cross(tile_turn, tile_len, query, grad_out, vision, w_key, w_value, text_turn, q_gain, k_gain):
    vmem = pl.BlockSpec(memory_space=pltpu.VMEM)
    hbm = pl.BlockSpec(memory_space=pltpu.HBM)
    rows, columns = query.shape
    heads = columns // HD
    width = vision.shape[1]
    return pl.pallas_call(
        cross_kernel,
        out_shape=(
            jax.ShapeDtypeStruct(query.shape, BF),
            jax.ShapeDtypeStruct(query.shape, BF),
            jax.ShapeDtypeStruct((CHUNK, width), BF),
            jax.ShapeDtypeStruct((width, HD), F32),
            jax.ShapeDtypeStruct((width, HD), F32),
        ),
        in_specs=[hbm] * 10,
        out_specs=(vmem,) * 5,
        scratch_shapes=[
            pltpu.VMEM((rows, columns), BF),
            pltpu.VMEM((rows, columns), BF),
            pltpu.VMEM((NC, NY, CHUNK, width), BF),
            pltpu.VMEM((width, HD), BF),
            pltpu.VMEM((width, HD), BF),
            pltpu.VMEM((rows // HD, HD), jnp.int32),
            pltpu.VMEM((1, HD), F32),
            pltpu.VMEM((1, HD), F32),
            pltpu.SMEM((SLOTS // TILE_TOK,), jnp.int32),
            pltpu.SMEM((SLOTS // TILE_TOK,), jnp.int32),
            pltpu.SemaphoreType.DMA((10,)),
            pltpu.VMEM((heads, rows, 2 * HD), BF),
            pltpu.VMEM((heads, rows, 2 * HD), BF),
            pltpu.VMEM((SLOTS, 2 * HD), BF),
            pltpu.VMEM((SLOTS, 2 * HD), BF),
            pltpu.VMEM((heads, rows, 1), F32),
            pltpu.VMEM((heads, rows, SLOTS), BF),
            pltpu.VMEM((2, HD, SLOTS), F32),
            pltpu.VMEM((HD, 2 * HD), BF),
            pltpu.VMEM((width, SLOTS), BF),
            pltpu.VMEM((NY, CHUNK, NC * width), F32),
            pltpu.VMEM((2, NY, CHUNK, HD), BF),
            pltpu.VMEM((2, NY, CHUNK, HD), F32),
            pltpu.VMEM((SHARD, HD), F32),
            pltpu.VMEM((2, NC, NY, CHUNK, HD), BF),
            pltpu.VMEM((NY * NC, CHUNK, width), BF),
            pltpu.VMEM((NX, CHUNK, width), BF),
            pltpu.VMEM((2, NC, width, HD), BF),
            pltpu.VMEM((2, NC, width, HD), BF),
            pltpu.SemaphoreType.DMA((2,)),
            pltpu.SemaphoreType.DMA((2,)),
            pltpu.SemaphoreType.DMA((2,)),
            pltpu.SemaphoreType.REGULAR,
            pltpu.SemaphoreType.REGULAR,
            pltpu.SemaphoreType.REGULAR,
        ]
        + (scatter_scratch() + gather_scratch()) * 2
        + foreign_scratch(),
        compiler_params=pltpu.CompilerParams(collective_id=0, has_side_effects=True, vmem_limit_bytes=VMEM_LIMIT),
        name="cross",
    )(
        *(
            pltpu.with_memory_space_constraint(operand, pltpu.HBM)
            for operand in (
                tile_turn, tile_len, query, grad_out, vision.reshape(NC, NY, CHUNK, width), w_key, w_value, text_turn,
                q_gain, k_gain,
            )
        )
    )


def emit_kernel(*refs):
    count = len(refs) // 2
    copies = []
    for i in range(count):
        for start in range(0, refs[i].shape[0], CHUNK):
            part = pl.ds(start, CHUNK)
            copies.append(pltpu.make_async_copy(refs[i].at[part], refs[count + i].at[part], refs[-1].at[len(copies)]))
    for copy in copies:
        copy.start()
    for copy in copies:
        copy.wait()


def emit(arrays):
    vmem = pl.BlockSpec(memory_space=pltpu.VMEM)
    hbm = pl.BlockSpec(memory_space=pltpu.HBM)
    return pl.pallas_call(
        emit_kernel,
        out_shape=tuple(jax.ShapeDtypeStruct(a.shape, a.dtype) for a in arrays),
        in_specs=[vmem] * len(arrays),
        out_specs=(hbm,) * len(arrays),
        scratch_shapes=[pltpu.SemaphoreType.DMA((sum(a.shape[0] // CHUNK for a in arrays),))],
        compiler_params=pltpu.CompilerParams(vmem_limit_bytes=8 * 1024 * 1024),
        name="emit",
    )(*arrays)


def body(query, vision, w_key, w_value, q_gain, k_gain, text_turn, tile_turn, tile_len, grad_out):
    outs = cross(
        tile_turn, tile_len, query, grad_out, vision, w_key, w_value,
        text_turn.reshape(-1, HD), q_gain.reshape(1, HD), k_gain.reshape(1, HD),
    )
    return emit(outs)


def solution(mesh):
    return jax.shard_map(
        body,
        mesh=mesh,
        in_specs=(
            P("turn", "head"),
            P(None, "turn"),
            P("turn", "head"),
            P("turn", "head"),
            P(),
            P(),
            P("turn"),
            P(),
            P(),
            P("turn", "head"),
        ),
        out_specs=(
            P("turn", "head"),
            P("turn", "head"),
            P("head", "turn"),
            P("turn", "head"),
            P("turn", "head"),
        ),
        check_vma=False,
    )
```
